512 devices in a mesh: tgt: 128 (over x, z, y_hi, core), src: 4 (over y_lo).
Axes of the slice: x: 4, y: 8 (y_hi: 2, y_lo: 4; y = y_hi * 4 + y_lo), z: 8, core: 2. Of those that a mesh axis runs over, the one named last changes fastest.
Arguments:
- fibre_points: float32 [3, 1024, 64], P(None, ('tgt', 'src')), may hold values from -6 to 6
- shell_points: float32 [3, 128, 64], P(None, 'tgt', 'src'), may hold values from -7 to 7, as said below
- bending: float32 [64, 64], replicated, may hold values from -0.12 to 0.12
- shell_inverse: bfloat16 [3, 128, 64, 3, 64, 128], P(None, 'tgt', None, None, 'src'), may hold values from -0.0390625 to 0.0390625
Outputs:
- fibre_velocity: float32 [3, 1024, 64], P(None, ('tgt', 'src'))
- shell_density: float32 [3, 128, 64], P(None, 'tgt', 'src')
The draws below stay inside these ranges and needn't reach their ends.
Inputs may be any that keep to these rules, and one draw needn't show every extreme that they name: `shell_points`: every shell node lies on the sphere of radius 7 about the anchor.
All inputs are finite; a program needn't handle non-finite values.
Results may differ from the reference program's by a relative error of at most 0.0029.
Values may be sent and summed in bfloat16 or wider, within the bound.
No kernel may reach another device: no remote copies, remote signals or barrier semaphores. Data moves between devices by JAX's collectives and lax.ppermute only.
A program may use at most 64 MiB of HBM per device.

```python
import math
import jax
import jax.numpy as jnp
from jax import lax

NODES = 64
NSA = 128
NSB = 64
ITERS = 1
FIBRES = 1024
SHELL = 8192


def draw_shell_points(key, part):
    height_key, angle_key = jax.random.split(key)
    height = jax.random.uniform(height_key, (NSA, NSB), jnp.float32, -1.0, 1.0)
    angle = jax.random.uniform(angle_key, (NSA, NSB), jnp.float32, -math.pi, math.pi)
    radial = jnp.sqrt(jnp.maximum(1.0 - height * height, 0.0))
    return 7.0 * jnp.stack([radial * jnp.cos(angle), radial * jnp.sin(angle), height])


def steps_of(own_key, extent, cuts, smallest, top_value):
    def one(dim, parts):
        steps = jax.random.uniform(jax.random.fold_in(jax.random.fold_in(own_key, 6), dim), (parts,), jnp.float32, smallest / len(cuts), top_value / len(cuts))
        return jnp.repeat(jnp.exp(steps), extent[dim] // parts).reshape((-1,) + (1,) * (len(extent) - dim - 1))

    loudness = one(*cuts[0])
    for cut in cuts[1:]:
        loudness = loudness * one(*cut)
    return loudness


def bell_draw(key, extent, spread, bound, cuts=(), dtype=jnp.bfloat16):
    factor_of = steps_of(key, extent, cuts, -0.22, 0.18) if cuts else 1.0
    drawn = jax.random.normal(key, extent, jnp.float32) * spread * factor_of
    return jnp.minimum(jnp.maximum(drawn, -bound), bound).astype(dtype)


def setup_inputs(seed: int = 0) -> dict:
    keys = jax.random.split(jax.random.key(seed), 5)
    return {
        "fibre_points": bell_draw(keys[0], (3, FIBRES, NODES), 1.0, 6.0, ((1, 512),), jnp.float32),
        "shell_points": draw_shell_points(jax.random.fold_in(keys[4], 71), 0),
        "bending": bell_draw(keys[2], (NODES, NODES), 0.02, 0.12, (), jnp.float32),
        "shell_inverse": bell_draw(keys[3], (3, NSA, NSB, 3, NSB, NSA), (3 * SHELL) ** -0.5, 0.0390625, ((1, 128), (4, 4))),
    }


mobility = 1.0 / (8.0 * math.pi)
soften_sq = 0.0025
time_step = 0.5

def stokes_flow(targets, sources, strength):
    delta_x = targets[0][:, None] - sources[0][None, :]
    delta_y = targets[1][:, None] - sources[1][None, :]
    delta_z = targets[2][:, None] - sources[2][None, :]
    dist_sq = delta_x * delta_x + delta_y * delta_y + delta_z * delta_z
    inv_root = lax.rsqrt(dist_sq + soften_sq)
    inv_cubed = inv_root * inv_root * inv_root
    projection = (delta_x * strength[0][None, :] + delta_y * strength[1][None, :] + delta_z * strength[2][None, :]) * inv_cubed
    diagonal_part = (dist_sq + 2.0 * soften_sq) * inv_cubed
    flow_x = lax.optimization_barrier(jnp.sum(diagonal_part * strength[0][None, :] + projection * delta_x, axis=1))
    flow_y = lax.optimization_barrier(jnp.sum(diagonal_part * strength[1][None, :] + projection * delta_y, axis=1))
    flow_z = lax.optimization_barrier(jnp.sum(diagonal_part * strength[2][None, :] + projection * delta_z, axis=1))
    return mobility * jnp.stack([flow_x, flow_y, flow_z])

def blocked_flow(targets, sources, strength):
    column_count = targets.shape[1]
    block_size = math.gcd(column_count, 128)
    blocks = targets.reshape(3, column_count // block_size, block_size).transpose(1, 0, 2)

    def one_block(target_block):
        return stokes_flow(target_block, sources, strength)
    result = lax.map(one_block, blocks)
    return result.transpose(1, 0, 2).reshape(3, column_count)

def reference(fibre_points, shell_points, bending, shell_inverse):
    points = fibre_points
    shell_flat = shell_points.reshape(3, -1)
    matrix = shell_inverse.reshape(3 * SHELL, 3 * SHELL)
    fibre_count = FIBRES * NODES
    velocity = jnp.zeros(points.shape, jnp.float32)
    density = jnp.zeros(shell_points.shape, jnp.float32)
    for iteration in range(ITERS):
        forces = -jnp.einsum('cfm,nm->cfn', points, bending, precision=lax.Precision.HIGHEST)
        sources = points.reshape(3, -1)
        targets = jnp.concatenate([sources, shell_flat], axis=1)
        flow_all = blocked_flow(targets, sources, forces.reshape(3, -1))
        fibre_flow = flow_all[:, :fibre_count].reshape(points.shape)
        shell_flow = flow_all[:, fibre_count:].reshape(3, NSA, NSB)
        columns = shell_flow.astype(jnp.bfloat16).transpose(0, 2, 1).reshape(-1)
        density = -jnp.dot(matrix, columns, preferred_element_type=jnp.float32).reshape(3, NSA, NSB)
        shell_back = blocked_flow(sources, shell_flat, density.reshape(3, -1)).reshape(points.shape)
        velocity = fibre_flow + shell_back
        if iteration + 1 < ITERS:
            points = points + time_step * velocity
    return (velocity, density)
```

```python
import math

import jax
import jax.numpy as jnp
from jax import lax
from jax.experimental import pallas as pl
from jax.experimental.pallas import tpu as pltpu
from jax.sharding import Mesh
from jax.sharding import PartitionSpec as P

AXES = ("tgt_0", "tgt_1", "tgt_2", "tgt_3", "src")
TGT = AXES[:4]
LINE = ("tgt_2", "tgt_3", "src")
PLANE = ("tgt_0", "tgt_1")
N_LINE = 16
N_PLANE = 32
SOURCES = N_PLANE * 128
SHELL_SOURCES = N_PLANE * 16
CHUNKS = 4
STEP = 512

F32 = jnp.float32
BF16 = jnp.bfloat16
scale = 20.0
mobility = scale / (8.0 * math.pi)


def three_parts(x):
    high = x.astype(BF16).astype(F32)
    rest = x - high
    middle = rest.astype(BF16).astype(F32)
    low = (rest - middle).astype(BF16).astype(F32)
    return high, middle, low


def left_rows(x):
    a, b, c = three_parts(x)
    return jnp.concatenate([a, a, b, b, a, c], axis=0).astype(BF16)


def right_rows(x):
    a, b, c = three_parts(x)
    return jnp.concatenate([a, b, a, b, c, a], axis=0).T.astype(BF16)


def rows_of(x):
    return lax.broadcasted_iota(jnp.int32, x.shape, 0)


def source_features(places, pushes):
    row = rows_of(places)
    places = jnp.where(row < 3, places * scale, 0.0)
    pushes = jnp.where(row < 3, pushes, 0.0)
    square = jnp.sum(places * places, axis=0, keepdims=True)
    along = jnp.sum(places * pushes, axis=0, keepdims=True)
    dist = jnp.where(row < 3, -2.0 * places, jnp.where(row == 3, 1.0, jnp.where(row == 4, square, 0.0)))
    proj = jnp.where(row == 4, -along, pushes)
    a, b, _ = three_parts(pushes)
    push_rows = jnp.concatenate([a, b], axis=0).astype(BF16)
    a, b, c = three_parts(jnp.where(row == 3, 1.0, places))
    place_rows = jnp.concatenate([a, b, c, jnp.zeros_like(a)], axis=0).astype(BF16)
    return right_rows(dist), right_rows(proj), push_rows, place_rows


def pair_sums(targets, count, dist_ref, proj_ref, push_ref, place_ref, unroll, fine):
    row = rows_of(targets)
    x = jnp.where(row < 3, targets * scale, 0.0)
    square = jnp.sum(x * x, axis=0, keepdims=True) + 1.0
    features = left_rows(jnp.where(row == 3, square, jnp.where(row == 4, 1.0, x)))
    width = targets.shape[1]
    step = min(STEP, count)

    def add_block(k, sums):
        diag_sum, proj_sum = sums
        part = pl.ds(pl.multiple_of(k * step, step), step)
        dist_sq = jnp.dot(dist_ref[part, :], features, preferred_element_type=F32)
        along = jnp.dot(proj_ref[part, :], features, preferred_element_type=F32)
        inv_root = lax.rsqrt(dist_sq)
        inv_cubed = inv_root * inv_root * inv_root
        diag = inv_root + inv_cubed
        high = diag.astype(BF16)
        low = (diag - high.astype(F32)).astype(BF16)
        diag_sum += jnp.dot(push_ref[:, part], high, preferred_element_type=F32)
        diag_sum += jnp.dot(push_ref[:, part], low, preferred_element_type=F32)
        proj = along * inv_cubed
        high = proj.astype(BF16)
        proj_sum += jnp.dot(place_ref[:, part], high, preferred_element_type=F32)
        if fine:
            low = (proj - high.astype(F32)).astype(BF16)
            proj_sum += jnp.dot(place_ref[:, part], low, preferred_element_type=F32)
        return diag_sum, proj_sum

    start = (jnp.zeros((16, width), F32), jnp.zeros((32, width), F32))
    diag_sum, proj_sum = lax.fori_loop(0, count // step, add_block, start, unroll=unroll)
    moved = proj_sum[0:8] + proj_sum[8:16] + proj_sum[16:24]
    return (diag_sum[0:8] + diag_sum[8:16] + x * moved[3:4] - moved) * mobility


def side_by_side(ref, first, count):
    return jnp.concatenate([ref[first + i] for i in range(count)], axis=1)


def packed(tiles, first_row):
    row = rows_of(tiles[0])
    lane = lax.broadcasted_iota(jnp.int32, tiles[0].shape, 1)
    keep = (row >= first_row) & (row < first_row + 3) & (lane < 16)
    blocks = []
    for start in range(0, len(tiles), 8):
        block = jnp.zeros_like(tiles[0])
        for i, tile in enumerate(tiles[start : start + 8]):
            piece = jnp.where(keep, tile, 0.0)
            block += pltpu.roll(piece, 16 * i, 1) if i else piece
        blocks.append(pltpu.roll(block, 8 - first_row, 0) if first_row else block)
    return jnp.concatenate(blocks, axis=1)


def own_kernel(fibre_ref, shell_ref, line_ref, plane_ref):
    fibre = jnp.concatenate([fibre_ref[:, 0, :], fibre_ref[:, 1, :]], axis=1)
    shell = jnp.concatenate([shell_ref[:, 0, :], jnp.zeros((3, 112), F32)], axis=1)
    tile = jnp.concatenate([fibre, shell, jnp.zeros((2, 128), F32)], axis=0)
    line_ref[...] = jnp.broadcast_to(tile[None], line_ref.shape)
    plane_ref[...] = jnp.broadcast_to(tile[None], plane_ref.shape)


def shell_kernel(line_ref, plane_ref, bending_ref, part_ref, dist_ref, proj_ref, push_ref, place_ref, shell_ref):
    square = bending_ref[...]
    zero = jnp.zeros_like(square)
    both = jnp.concatenate(
        [jnp.concatenate([square, zero], axis=1), jnp.concatenate([zero, square], axis=1)], axis=0
    )
    places = plane_ref[...].reshape(N_PLANE * 8, 128)
    pushes = -lax.dot_general(
        places, both, (((1,), (1,)), ((), ())), precision=lax.Precision.HIGHEST, preferred_element_type=F32
    )
    pushes = jnp.concatenate([pushes[8 * i : 8 * i + 8] for i in range(N_PLANE)], axis=1)
    places = side_by_side(plane_ref, 0, N_PLANE)
    dist_ref[...], proj_ref[...], push_ref[...], place_ref[...] = source_features(places, pushes)
    shell_ref[...] = packed([plane_ref[i] for i in range(N_PLANE)], 3)
    order = [pair * 4 + src for src in range(4) for pair in range(4)]
    targets = packed([line_ref[i] for i in order], 3)
    flow = pair_sums(targets, SOURCES, dist_ref, proj_ref, push_ref, place_ref, 4, True)
    for src in range(4):
        half = flow[:, 128 * (src // 2) : 128 * (src // 2) + 128]
        piece = pltpu.roll(half, 64, 1) if src % 2 else half
        for pair in range(4):
            part_ref[pair * 4 + src] = piece


def fibre_kernel(line_ref, dist_ref, proj_ref, push_ref, place_ref, flow_ref):
    count = N_LINE // CHUNKS
    flow = pair_sums(
        side_by_side(line_ref, 0, count), SOURCES, dist_ref, proj_ref, push_ref, place_ref, 4, False
    )
    for i in range(count):
        flow_ref[i] = flow[:, 128 * i : 128 * i + 128]


def sum_kernel(parts_ref, out_ref):
    total = parts_ref[0]
    for i in range(1, parts_ref.shape[0]):
        total += parts_ref[i]
    out_ref[...] = jnp.broadcast_to(total[None], out_ref.shape)


def back_kernel(line_ref, shell_ref, density_ref, *refs):
    flows, (part_ref, dist_ref, proj_ref, push_ref, place_ref) = refs[:CHUNKS], refs[CHUNKS:]
    pushes = packed([density_ref[i] for i in range(N_PLANE)], 0)
    dist_ref[...], proj_ref[...], push_ref[...], place_ref[...] = source_features(shell_ref[...], pushes)
    count = N_LINE // CHUNKS
    for chunk in range(CHUNKS):
        flow = pair_sums(
            side_by_side(line_ref, chunk * count, count),
            SHELL_SOURCES,
            dist_ref,
            proj_ref,
            push_ref,
            place_ref,
            1,
            False,
        )
        for i in range(count):
            part_ref[chunk * count + i] = flow[:, 128 * i : 128 * i + 128] + flows[chunk][i]


def tiles(count):
    return jax.ShapeDtypeStruct((count, 8, 128), F32)


def cost(pairs):
    return pl.CostEstimate(flops=pairs * 400, bytes_accessed=1 << 20, transcendentals=pairs)


def params():
    return pltpu.CompilerParams(vmem_limit_bytes=24 << 20)


def feature_shapes(count):
    return [((count, 48), BF16), ((count, 48), BF16), ((16, count), BF16), ((32, count), BF16)]


def exchange(x, axes):
    return lax.all_to_all(x, axes, 0, 0, tiled=True)


def per_device(fibre_points, shell_points, bending, shell_inverse):
    own_line, own_plane = pl.pallas_call(own_kernel, out_shape=[tiles(N_LINE), tiles(N_PLANE)])(
        fibre_points, shell_points
    )
    plane = exchange(own_plane, PLANE)
    line = exchange(own_line, LINE)
    features = [jax.ShapeDtypeStruct(s, t) for s, t in feature_shapes(SOURCES)]
    shell_part, *features, shell_places = pl.pallas_call(
        shell_kernel,
        out_shape=[tiles(N_LINE), *features, jax.ShapeDtypeStruct((8, SHELL_SOURCES), F32)],
        compiler_params=params(),
        cost_estimate=cost(256 * SOURCES),
    )(line, plane, bending)
    count = N_LINE // CHUNKS

    def fibre_chunk(chunk, after):
        held, _ = lax.optimization_barrier((line, after))
        return pl.pallas_call(
            fibre_kernel,
            out_shape=tiles(count),
            grid=(1,),
            in_specs=[pl.BlockSpec((count, 8, 128), lambda i: (chunk, 0, 0))]
            + [pl.BlockSpec(s, lambda i: (0, 0)) for s, _ in feature_shapes(SOURCES)],
            out_specs=pl.BlockSpec((count, 8, 128), lambda i: (0, 0, 0)),
            compiler_params=params(),
            cost_estimate=cost(count * 128 * SOURCES),
        )(held, *features)

    flows = []

    def exchange_beside(x, axes):
        flow = fibre_chunk(len(flows), x)
        x, flow = lax.optimization_barrier((exchange(x, axes), flow))
        flows.append(flow)
        return x

    shell_parts = exchange_beside(shell_part, LINE)
    shell_own = pl.pallas_call(sum_kernel, out_shape=tiles(N_PLANE))(shell_parts)
    shell_all = exchange_beside(shell_own, PLANE)
    columns = shell_all[:, :3, :64].astype(BF16).reshape(N_PLANE, 3, 4, 16)
    columns = columns.transpose(1, 3, 0, 2).reshape(3, 16, 128)
    density_rows = -jnp.einsum(
        "xaqcbn,cbn->xaq", shell_inverse, columns, preferred_element_type=F32
    )
    pieces = density_rows.reshape(3, 4, 16).transpose(1, 0, 2)
    pieces = jnp.pad(pieces, ((0, 0), (0, 5), (0, 112)))
    density_own = pl.pallas_call(sum_kernel, out_shape=tiles(N_PLANE))(exchange_beside(pieces, "src"))
    density = density_own[0, :3, None, :16]
    density_all = exchange_beside(density_own, PLANE)
    part = pl.pallas_call(
        back_kernel,
        out_shape=tiles(N_LINE),
        scratch_shapes=[pltpu.VMEM(s, t) for s, t in feature_shapes(SHELL_SOURCES)],
        compiler_params=params(),
        cost_estimate=cost(N_LINE * 128 * SHELL_SOURCES),
    )(line, shell_places, density_all, *flows)
    velocity = jnp.sum(exchange(part, LINE)[:, :3], axis=0)
    return velocity.reshape(3, 2, 64), density


def solution(mesh):
    torus = Mesh(mesh.devices.reshape(4, 8, 2, 2, mesh.shape["src"]), AXES)
    in_specs = (P(None, AXES, None), P(None, TGT, "src"), P(), P(None, TGT, None, None, "src", None))
    out_specs = (P(None, AXES, None), P(None, TGT, "src"))
    return jax.shard_map(per_device, mesh=torus, in_specs=in_specs, out_specs=out_specs, check_vma=False)
```

```python
import math

import jax
import jax.numpy as jnp
from jax import lax
from jax.experimental import pallas as pl
from jax.experimental.pallas import tpu as pltpu
from jax.sharding import Mesh
from jax.sharding import PartitionSpec as P

AXES = ("tgt_0", "tgt_1", "tgt_2", "tgt_3", "src")
TGT = AXES[:4]
LINE = ("tgt_2", "tgt_3", "src")
PLANE = ("tgt_0", "tgt_1")
N_LINE = 16
N_PLANE = 32
SOURCES = N_PLANE * 128
SHELL_SOURCES = N_PLANE * 16
CHUNKS = 4
STEP = 512
ROWS = (((0,), (0,)), ((), ()))

F32 = jnp.float32
BF16 = jnp.bfloat16
scale = 20.0
mobility = scale / (8.0 * math.pi)


def three_parts(x):
    high = x.astype(BF16).astype(F32)
    rest = x - high
    middle = rest.astype(BF16).astype(F32)
    low = (rest - middle).astype(BF16).astype(F32)
    return high, middle, low


def rows_of(x):
    return lax.broadcasted_iota(jnp.int32, x.shape, 0)


def left_rows(x, level):
    row = rows_of(x)
    a, b, c = three_parts(x)
    p, q, r = three_parts(level)
    first = jnp.where(row < 3, a, jnp.where(row == 3, p, jnp.where(row == 4, q, jnp.where(row == 5, r, 1.0))))
    second = jnp.where(row < 3, a, jnp.where(row == 3, 1.0, pltpu.roll(b, 4, 0)))
    return jnp.concatenate([first, second, b + pltpu.roll(a, 4, 0), c], axis=0).astype(BF16)


def right_rows(x, ones, level):
    row = rows_of(x)
    a, b, c = three_parts(x)
    p, q, r = three_parts(level)
    first = jnp.where(row < 3, a, jnp.where(row < 6, ones, jnp.where(row == 6, p, q)))
    second = jnp.where(row < 3, b, jnp.where(row == 3, r, pltpu.roll(a, 4, 0)))
    return jnp.concatenate([first, second, b + pltpu.roll(c, 4, 0), a], axis=0).astype(BF16)


def source_features(places, pushes):
    row = rows_of(places)
    places = jnp.where(row < 3, places * scale, 0.0)
    pushes = jnp.where(row < 3, pushes, 0.0)
    square = jnp.sum(places * places, axis=0, keepdims=True)
    along = jnp.sum(places * pushes, axis=0, keepdims=True)
    a, b, _ = three_parts(pushes)
    push_rows = jnp.concatenate([a, b], axis=0).astype(BF16)
    a, b, c = three_parts(jnp.where(row == 3, 1.0, places))
    place_rows = jnp.concatenate([a, b + pltpu.roll(c, 4, 0)], axis=0).astype(BF16)
    return right_rows(-2.0 * places, 1.0, square), right_rows(pushes, 0.0, -along), push_rows, place_rows


def pair_sums(targets, count, dist_ref, proj_ref, push_ref, place_ref, unroll, fine):
    row = rows_of(targets)
    x = jnp.where(row < 3, targets * scale, 0.0)
    square = jnp.sum(x * x, axis=0, keepdims=True) + 1.0
    features = left_rows(x, square)
    width = targets.shape[1]
    step = min(STEP, count)

    def add_block(k, sums):
        diag_sum, proj_sum = sums
        part = pl.ds(pl.multiple_of(k * step, step), step)
        dist_sq = lax.dot_general(dist_ref[:, part], features, ROWS, preferred_element_type=F32)
        along = lax.dot_general(proj_ref[:, part], features, ROWS, preferred_element_type=F32)
        inv_root = lax.rsqrt(dist_sq)
        inv_cubed = inv_root * inv_root * inv_root
        diag = inv_root + inv_cubed
        high = diag.astype(BF16)
        low = (diag - high.astype(F32)).astype(BF16)
        diag_sum += jnp.dot(push_ref[:, part], high, preferred_element_type=F32)
        diag_sum += jnp.dot(push_ref[:, part], low, preferred_element_type=F32)
        proj = along * inv_cubed
        high = proj.astype(BF16)
        proj_sum += jnp.dot(place_ref[:, part], high, preferred_element_type=F32)
        if fine:
            low = (proj - high.astype(F32)).astype(BF16)
            proj_sum += jnp.dot(place_ref[:, part], low, preferred_element_type=F32)
        return diag_sum, proj_sum

    start = (jnp.zeros((16, width), F32), jnp.zeros((16, width), F32))
    diag_sum, proj_sum = lax.fori_loop(0, count // step, add_block, start, unroll=unroll)
    rest = proj_sum[8:16]
    moved = proj_sum[0:8] + rest + pltpu.roll(rest, 4, 0)
    return (diag_sum[0:8] + diag_sum[8:16] + x * moved[3:4] - moved) * mobility


def side_by_side(ref, first, count):
    return jnp.concatenate([ref[first + i] for i in range(count)], axis=1)


def packed(tiles, first_row):
    row = rows_of(tiles[0])
    lane = lax.broadcasted_iota(jnp.int32, tiles[0].shape, 1)
    keep = (row >= first_row) & (row < first_row + 3) & (lane < 16)
    blocks = []
    for start in range(0, len(tiles), 8):
        block = jnp.zeros_like(tiles[0])
        for i, tile in enumerate(tiles[start : start + 8]):
            piece = jnp.where(keep, tile, 0.0)
            block += pltpu.roll(piece, 16 * i, 1) if i else piece
        blocks.append(pltpu.roll(block, 8 - first_row, 0) if first_row else block)
    return jnp.concatenate(blocks, axis=1)


def own_kernel(fibre_ref, shell_ref, line_ref, plane_ref):
    fibre = jnp.concatenate([fibre_ref[:, 0, :], fibre_ref[:, 1, :]], axis=1)
    shell = jnp.concatenate([shell_ref[:, 0, :], jnp.zeros((3, 112), F32)], axis=1)
    tile = jnp.concatenate([fibre, shell, jnp.zeros((2, 128), F32)], axis=0)
    line_ref[...] = jnp.broadcast_to(tile[None], line_ref.shape)
    plane_ref[...] = jnp.broadcast_to(tile[None], plane_ref.shape)


def source_kernel(plane_ref, bending_ref, dist_ref, proj_ref, push_ref, place_ref, shell_ref):
    square = bending_ref[...]
    zero = jnp.zeros_like(square)
    both = jnp.concatenate(
        [jnp.concatenate([square, zero], axis=1), jnp.concatenate([zero, square], axis=1)], axis=0
    )
    places = plane_ref[...].reshape(N_PLANE * 8, 128)
    pushes = -lax.dot_general(
        places, both, (((1,), (1,)), ((), ())), precision=lax.Precision.HIGHEST, preferred_element_type=F32
    )
    pushes = jnp.concatenate([pushes[8 * i : 8 * i + 8] for i in range(N_PLANE)], axis=1)
    places = side_by_side(plane_ref, 0, N_PLANE)
    dist_ref[...], proj_ref[...], push_ref[...], place_ref[...] = source_features(places, pushes)
    shell_ref[...] = packed([plane_ref[i] for i in range(N_PLANE)], 3)


def shell_kernel(line_ref, dist_ref, proj_ref, push_ref, place_ref, part_ref):
    order = [pair * 4 + src for src in range(4) for pair in range(4)]
    targets = packed([line_ref[i] for i in order], 3)
    flow = pair_sums(targets, SOURCES, dist_ref, proj_ref, push_ref, place_ref, 4, True)
    for src in range(4):
        half = flow[:, 128 * (src // 2) : 128 * (src // 2) + 128]
        piece = pltpu.roll(half, 64, 1) if src % 2 else half
        for pair in range(4):
            part_ref[pair * 4 + src] = piece


def fibre_kernel(line_ref, dist_ref, proj_ref, push_ref, place_ref, flow_ref):
    count = N_LINE // CHUNKS
    flow = pair_sums(
        side_by_side(line_ref, 0, count), SOURCES, dist_ref, proj_ref, push_ref, place_ref, 4, False
    )
    for i in range(count):
        flow_ref[i] = flow[:, 128 * i : 128 * i + 128]


def total_of(parts_ref):
    total = parts_ref[0]
    for i in range(1, parts_ref.shape[0]):
        total += parts_ref[i]
    return total


def columns_kernel(parts_ref, out_ref):
    total = total_of(parts_ref)
    total = jnp.concatenate([total, jnp.zeros_like(total)], axis=0).astype(BF16)
    out_ref[...] = jnp.broadcast_to(total[None], out_ref.shape)


def density_kernel(parts_ref, out_ref, density_ref):
    total = total_of(parts_ref)
    out_ref[...] = jnp.broadcast_to(total[None], out_ref.shape)
    density_ref[:, 0, :] = total[0:3, 0:16]


def velocity_kernel(parts_ref, out_ref):
    total = total_of(parts_ref)
    out_ref[:, 0, :] = total[0:3, 0:64]
    out_ref[:, 1, :] = total[0:3, 64:128]


def back_kernel(line_ref, shell_ref, density_ref, *refs):
    flows, (part_ref, dist_ref, proj_ref, push_ref, place_ref) = refs[:CHUNKS], refs[CHUNKS:]
    pushes = packed([density_ref[i] for i in range(N_PLANE)], 0)
    dist_ref[...], proj_ref[...], push_ref[...], place_ref[...] = source_features(shell_ref[...], pushes)
    count = N_LINE // CHUNKS
    for chunk in range(CHUNKS):
        flow = pair_sums(
            side_by_side(line_ref, chunk * count, count),
            SHELL_SOURCES,
            dist_ref,
            proj_ref,
            push_ref,
            place_ref,
            1,
            False,
        )
        for i in range(count):
            part_ref[chunk * count + i] = flow[:, 128 * i : 128 * i + 128] + flows[chunk][i]


def tiles(count):
    return jax.ShapeDtypeStruct((count, 8, 128), F32)


def cost(pairs):
    return pl.CostEstimate(flops=pairs * 400, bytes_accessed=1 << 20, transcendentals=pairs)


def params(mib):
    return pltpu.CompilerParams(vmem_limit_bytes=mib << 20)


def feature_shapes(count):
    return [((32, count), BF16), ((32, count), BF16), ((16, count), BF16), ((16, count), BF16)]


def exchange(x, axes):
    return lax.all_to_all(x, axes, 0, 0, tiled=True)


def per_device(fibre_points, shell_points, bending, shell_inverse):
    own_line, own_plane = pl.pallas_call(
        own_kernel, out_shape=[tiles(N_LINE), tiles(N_PLANE)], compiler_params=params(2)
    )(fibre_points, shell_points)
    plane = exchange(own_plane, PLANE)
    own_line, _ = lax.optimization_barrier((own_line, plane))
    features = [jax.ShapeDtypeStruct(s, t) for s, t in feature_shapes(SOURCES)]
    *features, shell_places = pl.pallas_call(
        source_kernel,
        out_shape=[*features, jax.ShapeDtypeStruct((8, SHELL_SOURCES), F32)],
        compiler_params=params(24),
        cost_estimate=cost(64 * SOURCES),
    )(plane, bending)
    line, features = lax.optimization_barrier((exchange(own_line, LINE), features))
    shell_part = pl.pallas_call(
        shell_kernel,
        out_shape=tiles(N_LINE),
        compiler_params=params(24),
        cost_estimate=cost(256 * SOURCES),
    )(line, *features)
    count = N_LINE // CHUNKS

    def fibre_chunk(chunk, after):
        held, _ = lax.optimization_barrier((line, after))
        return pl.pallas_call(
            fibre_kernel,
            out_shape=tiles(count),
            grid=(1,),
            in_specs=[pl.BlockSpec((count, 8, 128), lambda i: (chunk, 0, 0))]
            + [pl.BlockSpec(s, lambda i: (0, 0)) for s, _ in feature_shapes(SOURCES)],
            out_specs=pl.BlockSpec((count, 8, 128), lambda i: (0, 0, 0)),
            compiler_params=params(24),
            cost_estimate=cost(count * 128 * SOURCES),
        )(held, *features)

    flows = []

    def exchange_beside(x, axes):
        flow = fibre_chunk(len(flows), x)
        x, flow = lax.optimization_barrier((exchange(x, axes), flow))
        flows.append(flow)
        return x

    shell_parts = exchange_beside(shell_part, LINE)
    shell_own = pl.pallas_call(
        columns_kernel,
        out_shape=jax.ShapeDtypeStruct((N_PLANE, 16, 128), BF16),
        compiler_params=params(2),
    )(shell_parts)
    shell_all = exchange_beside(shell_own, PLANE)
    columns = shell_all[:, :3, :64].reshape(N_PLANE, 3, 4, 16)
    columns = columns.transpose(1, 3, 0, 2).reshape(3, 16, 128)
    density_rows = -jnp.einsum(
        "xaqcbn,cbn->xaq", shell_inverse, columns, preferred_element_type=F32
    )
    pieces = density_rows.reshape(3, 4, 16).transpose(1, 0, 2)
    pieces = jnp.pad(pieces, ((0, 0), (0, 5), (0, 112)))
    density_own, density = pl.pallas_call(
        density_kernel,
        out_shape=[tiles(N_PLANE), jax.ShapeDtypeStruct((3, 1, 16), F32)],
        compiler_params=params(2),
    )(exchange_beside(pieces, "src"))
    density_all = exchange_beside(density_own, PLANE)
    part = pl.pallas_call(
        back_kernel,
        out_shape=tiles(N_LINE),
        scratch_shapes=[pltpu.VMEM(s, t) for s, t in feature_shapes(SHELL_SOURCES)],
        compiler_params=params(24),
        cost_estimate=cost(N_LINE * 128 * SHELL_SOURCES),
    )(line, shell_places, density_all, *flows)
    velocity = pl.pallas_call(
        velocity_kernel, out_shape=jax.ShapeDtypeStruct((3, 2, 64), F32), compiler_params=params(2)
    )(exchange(part, LINE))
    return velocity, density


def solution(mesh):
    torus = Mesh(mesh.devices.reshape(4, 8, 2, 2, mesh.shape["src"]), AXES)
    in_specs = (P(None, AXES, None), P(None, TGT, "src"), P(), P(None, TGT, None, None, "src", None))
    out_specs = (P(None, AXES, None), P(None, TGT, "src"))
    return jax.shard_map(per_device, mesh=torus, in_specs=in_specs, out_specs=out_specs, check_vma=False)
```

```python
import functools
import math

import jax
import jax.numpy as jnp
from jax import lax
from jax.experimental import pallas as pl
from jax.experimental.pallas import tpu as pltpu
from jax.sharding import Mesh
from jax.sharding import PartitionSpec as P

AXES = ("tgt_0", "tgt_1", "tgt_2", "tgt_3", "src")
TGT = AXES[:4]
LINE = ("tgt_2", "tgt_3", "src")
PLANE = ("tgt_0", "tgt_1")
N_LINE = 16
N_PLANE = 32
SOURCES = N_PLANE * 128
SHELL = 8192
CHUNKS = ((0, (512, 256)), (6, (512, 512, 256)))
STEP = 512
ROWS = (((0,), (0,)), ((), ()))

F32 = jnp.float32
BF16 = jnp.bfloat16
scale = 20.0
mobility = scale / (8.0 * math.pi)


def three_parts(x):
    high = x.astype(BF16).astype(F32)
    rest = x - high
    middle = rest.astype(BF16).astype(F32)
    low = (rest - middle).astype(BF16).astype(F32)
    return high, middle, low


def rows_of(x):
    return lax.broadcasted_iota(jnp.int32, x.shape, 0)


def left_rows(x, level):
    row = rows_of(x)
    a, b, c = three_parts(x)
    p, q, r = three_parts(level)
    first = jnp.where(row < 3, a, jnp.where(row == 3, p, jnp.where(row == 4, q, jnp.where(row == 5, r, 1.0))))
    second = jnp.where(row < 3, a, jnp.where(row == 3, 1.0, pltpu.roll(b, 4, 0)))
    return jnp.concatenate([first, second, b + pltpu.roll(a, 4, 0), c], axis=0).astype(BF16)


def right_rows(x, ones, level):
    row = rows_of(x)
    a, b, c = three_parts(x)
    p, q, r = three_parts(level)
    first = jnp.where(row < 3, a, jnp.where(row < 6, ones, jnp.where(row == 6, p, q)))
    second = jnp.where(row < 3, b, jnp.where(row == 3, r, pltpu.roll(a, 4, 0)))
    return jnp.concatenate([first, second, b + pltpu.roll(c, 4, 0), a], axis=0).astype(BF16)


def source_features(places, pushes):
    row = rows_of(places)
    places = jnp.where(row < 3, places * scale, 0.0)
    pushes = jnp.where(row < 3, pushes, 0.0)
    square = jnp.sum(places * places, axis=0, keepdims=True)
    along = jnp.sum(places * pushes, axis=0, keepdims=True)
    a, b, _ = three_parts(pushes)
    push_rows = jnp.concatenate([a, b], axis=0).astype(BF16)
    a, b, c = three_parts(jnp.where(row == 3, 1.0, places))
    place_rows = jnp.concatenate([a, b + pltpu.roll(c, 4, 0)], axis=0).astype(BF16)
    return right_rows(-2.0 * places, 1.0, square), right_rows(pushes, 0.0, -along), push_rows, place_rows


def pair_sums(targets, count, dist_ref, proj_ref, push_ref, place_ref, unroll, fine, halves=False):
    row = rows_of(targets)
    x = jnp.where(row < 3, targets * scale, 0.0)
    square = jnp.sum(x * x, axis=0, keepdims=True) + 1.0
    features = left_rows(x, square)
    if halves:
        zero = jnp.zeros_like(features)
        features = jnp.concatenate(
            [jnp.concatenate([features, zero], axis=1), jnp.concatenate([zero, features], axis=1)], axis=0
        )
    width = features.shape[1]
    rows = push_ref.shape[0]
    step = min(STEP, count)

    def add_block(k, sums):
        diag_sum, proj_sum = sums
        part = pl.ds(pl.multiple_of(k * step, step), step)
        dist_sq = lax.dot_general(dist_ref[:, part], features, ROWS, preferred_element_type=F32)
        along = lax.dot_general(proj_ref[:, part], features, ROWS, preferred_element_type=F32)
        inv_root = lax.rsqrt(dist_sq)
        inv_cubed = inv_root * inv_root * inv_root
        diag = inv_root + inv_cubed
        high = diag.astype(BF16)
        low = (diag - high.astype(F32)).astype(BF16)
        diag_sum += jnp.dot(push_ref[:, part], high, preferred_element_type=F32)
        diag_sum += jnp.dot(push_ref[:, part], low, preferred_element_type=F32)
        proj = along * inv_cubed
        high = proj.astype(BF16)
        proj_sum += jnp.dot(place_ref[:, part], high, preferred_element_type=F32)
        if fine:
            low = (proj - high.astype(F32)).astype(BF16)
            proj_sum += jnp.dot(place_ref[:, part], low, preferred_element_type=F32)
        return diag_sum, proj_sum

    start = (jnp.zeros((rows, width), F32), jnp.zeros((rows, width), F32))
    diag_sum, proj_sum = lax.fori_loop(0, count // step, add_block, start, unroll=unroll)
    if halves:
        half = width // 2
        diag_sum = diag_sum[:16, :half] + diag_sum[16:, half:]
        proj_sum = proj_sum[:16, :half] + proj_sum[16:, half:]
    rest = proj_sum[8:16]
    moved = proj_sum[0:8] + rest + pltpu.roll(rest, 4, 0)
    return (diag_sum[0:8] + diag_sum[8:16] + x * moved[3:4] - moved) * mobility


def side_by_side(ref, first, count):
    return jnp.concatenate([ref[first + i] for i in range(count)], axis=1)


def packed(tiles, first_row):
    row = rows_of(tiles[0])
    lane = lax.broadcasted_iota(jnp.int32, tiles[0].shape, 1)
    keep = (row >= first_row) & (row < first_row + 3) & (lane < 16)
    blocks = []
    for start in range(0, len(tiles), 8):
        block = jnp.zeros_like(tiles[0])
        for i, tile in enumerate(tiles[start : start + 8]):
            piece = jnp.where(keep, tile, 0.0)
            block += pltpu.roll(piece, 16 * i, 1) if i else piece
        blocks.append(pltpu.roll(block, 8 - first_row, 0) if first_row else block)
    return jnp.concatenate(blocks, axis=1)


def own_kernel(fibre_ref, shell_ref, line_ref, plane_ref):
    fibre = jnp.concatenate([fibre_ref[:, 0, :], fibre_ref[:, 1, :]], axis=1)
    shell = jnp.concatenate([shell_ref[:, 0, :], jnp.zeros((3, 112), F32)], axis=1)
    tile = jnp.concatenate([fibre, shell, jnp.zeros((2, 128), F32)], axis=0)
    line_ref[...] = jnp.broadcast_to(tile[None], line_ref.shape)
    plane_ref[...] = jnp.broadcast_to(tile[None], plane_ref.shape)


def source_kernel(plane_ref, bending_ref, dist_ref, proj_ref, push_ref, place_ref):
    square = bending_ref[...]
    zero = jnp.zeros_like(square)
    both = jnp.concatenate(
        [jnp.concatenate([square, zero], axis=1), jnp.concatenate([zero, square], axis=1)], axis=0
    )
    places = plane_ref[...].reshape(N_PLANE * 8, 128)
    pushes = -lax.dot_general(
        places, both, (((1,), (1,)), ((), ())), precision=lax.Precision.HIGHEST, preferred_element_type=F32
    )
    pushes = jnp.concatenate([pushes[8 * i : 8 * i + 8] for i in range(N_PLANE)], axis=1)
    places = side_by_side(plane_ref, 0, N_PLANE)
    dist_ref[...], proj_ref[...], push_ref[...], place_ref[...] = source_features(places, pushes)


def shell_kernel(line_ref, dist_ref, proj_ref, push_ref, place_ref, part_ref, shell_ref):
    shell_ref[...] = packed([line_ref[i] for i in range(N_LINE)], 3)
    order = [pair * 4 + src for src in range(4) for pair in range(4)]
    targets = packed([line_ref[i] for i in order], 3)
    flow = pair_sums(targets, SOURCES, dist_ref, proj_ref, push_ref, place_ref, 4, True)
    for src in range(4):
        half = flow[:, 128 * (src // 2) : 128 * (src // 2) + 128]
        piece = pltpu.roll(half, 64, 1) if src % 2 else half
        for pair in range(4):
            part_ref[pair * 4 + src] = piece


def fibre_kernel(first, widths, line_ref, dist_ref, proj_ref, push_ref, place_ref, flow_ref):
    done = 0
    for width in widths:
        count = width // 128
        flow = pair_sums(
            side_by_side(line_ref, first + done, count),
            SOURCES,
            dist_ref,
            proj_ref,
            push_ref,
            place_ref,
            4,
            False,
        )
        for i in range(count):
            flow_ref[done + i] = flow[:, 128 * i : 128 * i + 128]
        done += count


def total_of(parts_ref):
    total = parts_ref[0]
    for i in range(1, parts_ref.shape[0]):
        total += parts_ref[i]
    return total


def columns_kernel(parts_ref, out_ref):
    total = total_of(parts_ref)
    total = jnp.concatenate([total, jnp.zeros_like(total)], axis=0).astype(BF16)
    out_ref[...] = jnp.broadcast_to(total[None], out_ref.shape)


def message_kernel(pair_ref, density_ref, *refs):
    flows, out_ref = refs[:-1], refs[-1]
    density = jnp.concatenate([density_ref[:, 0, :], jnp.zeros((3, 64), F32)], axis=1)
    density = jnp.concatenate([jnp.zeros((3, 128), F32), density, jnp.zeros((2, 128), F32)], axis=0)
    row = rows_of(density)
    lane = lax.broadcasted_iota(jnp.int32, density.shape, 1)
    pieces = []
    for src in range(4):
        own = jnp.where(lane // 16 == src, density, 0.0)
        pieces.append(pltpu.roll(own, 64 - 16 * src, 1))
    index = 0
    for flow_ref in flows:
        for i in range(flow_ref.shape[0]):
            mine = (pair_ref[0] == index // 4).astype(F32)
            out_ref[index] = jnp.where(row < 3, flow_ref[i], density + mine * pieces[index % 4])
            index += 1


def relay_kernel(parts_ref, shell_ref, out_ref, flow_ref, density_ref):
    lane = lax.broadcasted_iota(jnp.int32, (8, 128), 1)
    row = lax.broadcasted_iota(jnp.int32, (8, 128), 0)
    pairs = []
    for pair in range(4):
        total = parts_ref[pair * 4]
        for src in range(1, 4):
            total += parts_ref[pair * 4 + src]
        pairs.append(total)
    flow = (pairs[0] + pairs[1]) + (pairs[2] + pairs[3])
    flow_ref[...] = flow
    density_ref[:, 0, :] = flow[3:6, 64:80]
    places = shell_ref[...]
    for half in range(2):
        density = jnp.where(lane < 64, pairs[2 * half], pltpu.roll(pairs[2 * half + 1], 64, 1))
        density = pltpu.roll(density, 5, 0)
        place = pltpu.roll(places[:, 128 * half : 128 * half + 128], 3, 0)
        tile = jnp.where(row < 3, density, place)
        out_ref[:, :, 128 * half : 128 * half + 128] = jnp.broadcast_to(tile[None], (N_PLANE, 8, 128))


def back_kernel(own_ref, plane_ref, flow_ref, out_ref, dist_ref, proj_ref, push_ref, place_ref):
    for half in range(2):
        tile = side_by_side(plane_ref, half * (N_PLANE // 2), N_PLANE // 2)
        dist, proj, push, place = source_features(pltpu.roll(tile, 5, 0), tile)
        dist_ref[32 * half : 32 * half + 32] = dist
        proj_ref[32 * half : 32 * half + 32] = proj
        push_ref[16 * half : 16 * half + 16] = push
        place_ref[16 * half : 16 * half + 16] = place
    back = pair_sums(
        own_ref[0], SHELL // 2, dist_ref, proj_ref, push_ref, place_ref, 4, False, True
    )
    velocity = back + flow_ref[...]
    out_ref[:, 0, :] = velocity[0:3, 0:64]
    out_ref[:, 1, :] = velocity[0:3, 64:128]


def tiles(count):
    return jax.ShapeDtypeStruct((count, 8, 128), F32)


def cost(pairs):
    return pl.CostEstimate(flops=pairs * 400, bytes_accessed=1 << 20, transcendentals=pairs)


def params(mib):
    return pltpu.CompilerParams(vmem_limit_bytes=mib << 20)


def feature_shapes(count):
    return [((32, count), BF16), ((32, count), BF16), ((16, count), BF16), ((16, count), BF16)]


def exchange(x, axes):
    return lax.all_to_all(x, axes, 0, 0, tiled=True)


def per_device(fibre_points, shell_points, bending, shell_inverse):
    own_line, own_plane = pl.pallas_call(
        own_kernel, out_shape=[tiles(N_LINE), tiles(N_PLANE)], compiler_params=params(2)
    )(fibre_points, shell_points)
    plane = exchange(own_plane, PLANE)
    own_line, _ = lax.optimization_barrier((own_line, plane))
    features = [jax.ShapeDtypeStruct(s, t) for s, t in feature_shapes(SOURCES)]
    features = pl.pallas_call(
        source_kernel,
        out_shape=features,
        compiler_params=params(24),
        cost_estimate=cost(64 * SOURCES),
    )(plane, bending)
    line, features = lax.optimization_barrier((exchange(own_line, LINE), features))
    shell_part, shell_places = pl.pallas_call(
        shell_kernel,
        out_shape=[tiles(N_LINE), jax.ShapeDtypeStruct((8, 256), F32)],
        compiler_params=params(24),
        cost_estimate=cost(256 * SOURCES),
    )(line, *features)

    def fibre_chunk(chunk, after):
        held, _ = lax.optimization_barrier((line, after))
        first, widths = CHUNKS[chunk]
        return pl.pallas_call(
            functools.partial(fibre_kernel, first, widths),
            out_shape=tiles(sum(widths) // 128),
            compiler_params=params(24),
            cost_estimate=cost(sum(widths) * SOURCES),
        )(held, *features)

    flows = []

    def exchange_beside(x, axes):
        flow = fibre_chunk(len(flows), x)
        x, flow = lax.optimization_barrier((exchange(x, axes), flow))
        flows.append(flow)
        return x

    shell_parts = exchange_beside(shell_part, LINE)
    shell_own = pl.pallas_call(
        columns_kernel,
        out_shape=jax.ShapeDtypeStruct((N_PLANE, 16, 128), BF16),
        compiler_params=params(2),
    )(shell_parts)
    shell_all = exchange_beside(shell_own, PLANE)
    columns = shell_all[:, :3, :64].reshape(N_PLANE, 3, 4, 16)
    columns = columns.transpose(1, 3, 0, 2).reshape(3, 16, 128)
    density_rows = -jnp.einsum(
        "xaqcbn,cbn->xaq", shell_inverse, columns, preferred_element_type=F32
    )
    pair = lax.axis_index("tgt_2") * 2 + lax.axis_index("tgt_3")
    message = pl.pallas_call(
        message_kernel,
        out_shape=tiles(N_LINE),
        in_specs=[pl.BlockSpec(memory_space=pltpu.SMEM)] + [pl.BlockSpec(memory_space=pltpu.VMEM)] * 3,
        compiler_params=params(2),
    )(pair.astype(jnp.int32).reshape(1), density_rows, *flows)
    relay, fibre_flow, density = pl.pallas_call(
        relay_kernel,
        out_shape=[
            jax.ShapeDtypeStruct((N_PLANE, 8, 256), F32),
            jax.ShapeDtypeStruct((8, 128), F32),
            jax.ShapeDtypeStruct((3, 1, 16), F32),
        ],
        compiler_params=params(2),
    )(exchange(message, LINE), shell_places)
    velocity = pl.pallas_call(
        back_kernel,
        out_shape=jax.ShapeDtypeStruct((3, 2, 64), F32),
        scratch_shapes=[pltpu.VMEM((2 * s[0], SHELL // 2), t) for s, t in feature_shapes(0)],
        compiler_params=params(24),
    )(own_line, exchange(relay, PLANE), fibre_flow)
    return velocity, density


def solution(mesh):
    torus = Mesh(mesh.devices.reshape(4, 8, 2, 2, mesh.shape["src"]), AXES)
    in_specs = (P(None, AXES, None), P(None, TGT, "src"), P(), P(None, TGT, None, None, "src", None))
    out_specs = (P(None, AXES, None), P(None, TGT, "src"))
    return jax.shard_map(per_device, mesh=torus, in_specs=in_specs, out_specs=out_specs, check_vma=False)
```

```python
import functools
import math

import jax
import jax.numpy as jnp
from jax import lax
from jax.experimental import pallas as pl
from jax.experimental.pallas import tpu as pltpu
from jax.sharding import Mesh
from jax.sharding import PartitionSpec as P

AXES = ("tgt_0", "tgt_1", "tgt_2", "tgt_3", "src")
TGT = AXES[:4]
LINE = ("tgt_2", "tgt_3", "src")
PLANE = ("tgt_0", "tgt_1")
N_LINE = 16
N_PLANE = 32
SOURCES = N_PLANE * 128
BACK_SOURCES = N_PLANE * 64
CHUNKS = ((0, (512, 256)), (6, (512, 256)), (12, (512,)))
STEP = 512
ROWS = (((0,), (0,)), ((), ()))

F32 = jnp.float32
BF16 = jnp.bfloat16
scale = 20.0
mobility = scale / (8.0 * math.pi)


def three_parts(x):
    high = x.astype(BF16).astype(F32)
    rest = x - high
    middle = rest.astype(BF16).astype(F32)
    low = (rest - middle).astype(BF16).astype(F32)
    return high, middle, low


def rows_of(x):
    return lax.broadcasted_iota(jnp.int32, x.shape, 0)


def left_rows(x, level):
    row = rows_of(x)
    a, b, c = three_parts(x)
    p, q, r = three_parts(level)
    first = jnp.where(row < 3, a, jnp.where(row == 3, p, jnp.where(row == 4, q, jnp.where(row == 5, r, 1.0))))
    second = jnp.where(row < 3, a, jnp.where(row == 3, 1.0, pltpu.roll(b, 4, 0)))
    return jnp.concatenate([first, second, b + pltpu.roll(a, 4, 0), c], axis=0).astype(BF16)


def right_rows(x, ones, level):
    row = rows_of(x)
    a, b, c = three_parts(x)
    p, q, r = three_parts(level)
    first = jnp.where(row < 3, a, jnp.where(row < 6, ones, jnp.where(row == 6, p, q)))
    second = jnp.where(row < 3, b, jnp.where(row == 3, r, pltpu.roll(a, 4, 0)))
    return jnp.concatenate([first, second, b + pltpu.roll(c, 4, 0), a], axis=0).astype(BF16)


def source_features(places, pushes):
    row = rows_of(places)
    places = jnp.where(row < 3, places * scale, 0.0)
    pushes = jnp.where(row < 3, pushes, 0.0)
    square = jnp.sum(places * places, axis=0, keepdims=True)
    along = jnp.sum(places * pushes, axis=0, keepdims=True)
    a, b, _ = three_parts(pushes)
    push_rows = jnp.concatenate([a, b], axis=0).astype(BF16)
    a, b, c = three_parts(jnp.where(row == 3, 1.0, places))
    place_rows = jnp.concatenate([a, b + pltpu.roll(c, 4, 0)], axis=0).astype(BF16)
    return right_rows(-2.0 * places, 1.0, square), right_rows(pushes, 0.0, -along), push_rows, place_rows


def pair_sums(targets, count, dist_ref, proj_ref, push_ref, place_ref, unroll, level):
    row = rows_of(targets)
    x = jnp.where(row < 3, targets * scale, 0.0)
    square = jnp.sum(x * x, axis=0, keepdims=True) + 1.0
    features = left_rows(x, square)
    width = features.shape[1]
    step = min(STEP, count)

    def add_block(k, sums):
        diag_sum, proj_sum = sums
        part = pl.ds(pl.multiple_of(k * step, step), step)
        dist_sq = lax.dot_general(dist_ref[:, part], features, ROWS, preferred_element_type=F32)
        along = lax.dot_general(proj_ref[:, part], features, ROWS, preferred_element_type=F32)
        inv_root = lax.rsqrt(dist_sq)
        inv_cubed = inv_root * inv_root * inv_root
        diag = inv_root + inv_cubed
        high = diag.astype(BF16)
        diag_sum += jnp.dot(push_ref[:, part], high, preferred_element_type=F32)
        if level > 0:
            low = (diag - high.astype(F32)).astype(BF16)
            diag_sum += jnp.dot(push_ref[:, part], low, preferred_element_type=F32)
        proj = along * inv_cubed
        high = proj.astype(BF16)
        proj_sum += jnp.dot(place_ref[:, part], high, preferred_element_type=F32)
        if level > 1:
            low = (proj - high.astype(F32)).astype(BF16)
            proj_sum += jnp.dot(place_ref[:, part], low, preferred_element_type=F32)
        return diag_sum, proj_sum

    start = (jnp.zeros((16, width), F32), jnp.zeros((16, width), F32))
    diag_sum, proj_sum = lax.fori_loop(0, count // step, add_block, start, unroll=unroll)
    rest = proj_sum[8:16]
    moved = proj_sum[0:8] + rest + pltpu.roll(rest, 4, 0)
    return (diag_sum[0:8] + diag_sum[8:16] + x * moved[3:4] - moved) * mobility


def side_by_side(ref, first, count):
    return jnp.concatenate([ref[first + i] for i in range(count)], axis=1)


def packed(tiles, first_row):
    row = rows_of(tiles[0])
    lane = lax.broadcasted_iota(jnp.int32, tiles[0].shape, 1)
    keep = (row >= first_row) & (row < first_row + 3) & (lane < 16)
    blocks = []
    for start in range(0, len(tiles), 8):
        block = jnp.zeros_like(tiles[0])
        for i, tile in enumerate(tiles[start : start + 8]):
            piece = jnp.where(keep, tile, 0.0)
            block += pltpu.roll(piece, 16 * i, 1) if i else piece
        blocks.append(pltpu.roll(block, 8 - first_row, 0) if first_row else block)
    return jnp.concatenate(blocks, axis=1)


def own_kernel(fibre_ref, shell_ref, line_ref, plane_ref):
    fibre = jnp.concatenate([fibre_ref[:, 0, :], fibre_ref[:, 1, :]], axis=1)
    shell = jnp.concatenate([shell_ref[:, 0, :], jnp.zeros((3, 112), F32)], axis=1)
    tile = jnp.concatenate([fibre, shell, jnp.zeros((2, 128), F32)], axis=0)
    line_ref[...] = jnp.broadcast_to(tile[None], line_ref.shape)
    plane_ref[...] = jnp.broadcast_to(tile[None], plane_ref.shape)


def source_kernel(plane_ref, bending_ref, dist_ref, proj_ref, push_ref, place_ref):
    square = bending_ref[...]
    zero = jnp.zeros_like(square)
    both = jnp.concatenate(
        [jnp.concatenate([square, zero], axis=1), jnp.concatenate([zero, square], axis=1)], axis=0
    )
    places = plane_ref[...].reshape(N_PLANE * 8, 128)
    pushes = -lax.dot_general(
        places, both, (((1,), (1,)), ((), ())), precision=lax.Precision.HIGHEST, preferred_element_type=F32
    )
    pushes = jnp.concatenate([pushes[8 * i : 8 * i + 8] for i in range(N_PLANE)], axis=1)
    places = side_by_side(plane_ref, 0, N_PLANE)
    dist_ref[...], proj_ref[...], push_ref[...], place_ref[...] = source_features(places, pushes)


def shell_kernel(line_ref, dist_ref, proj_ref, push_ref, place_ref, part_ref, shell_ref):
    shell_ref[...] = packed([line_ref[i] for i in range(N_LINE)], 3)
    order = [pair * 4 + src for src in range(4) for pair in range(4)]
    targets = packed([line_ref[i] for i in order], 3)
    flow = pair_sums(targets, SOURCES, dist_ref, proj_ref, push_ref, place_ref, 4, 2)
    for src in range(4):
        half = flow[:, 128 * (src // 2) : 128 * (src // 2) + 128]
        piece = pltpu.roll(half, 64, 1) if src % 2 else half
        for pair in range(4):
            part_ref[pair * 4 + src] = piece


def fibre_kernel(first, widths, line_ref, dist_ref, proj_ref, push_ref, place_ref, flow_ref):
    done = 0
    for width in widths:
        count = width // 128
        flow = pair_sums(
            side_by_side(line_ref, first + done, count),
            SOURCES,
            dist_ref,
            proj_ref,
            push_ref,
            place_ref,
            4,
            1,
        )
        for i in range(count):
            flow_ref[done + i] = flow[:, 128 * i : 128 * i + 128]
        done += count


def total_of(parts_ref):
    total = parts_ref[0]
    for i in range(1, parts_ref.shape[0]):
        total += parts_ref[i]
    return total


def columns_kernel(parts_ref, out_ref):
    total = total_of(parts_ref)
    total = jnp.concatenate([total, jnp.zeros_like(total)], axis=0).astype(BF16)
    out_ref[...] = jnp.broadcast_to(total[None], out_ref.shape)


def density_kernel(pair_ref, density_ref, shell_ref, out_ref):
    density = jnp.concatenate([density_ref[:, 0, :], jnp.zeros((3, 64), F32)], axis=1)
    density = jnp.concatenate([density, jnp.zeros((5, 128), F32)], axis=0)
    lane = lax.broadcasted_iota(jnp.int32, density.shape, 1)
    places = jnp.zeros_like(density)
    for pair in range(4):
        half = shell_ref[:, 128 * (pair // 2) : 128 * (pair // 2) + 128]
        half = pltpu.roll(half, 64, 1) if pair % 2 else half
        places += jnp.where((pair_ref[0] == pair) & (lane < 64), half, 0.0)
    tile = density + pltpu.roll(places, 3, 0)
    out_ref[...] = jnp.broadcast_to(tile[None], out_ref.shape)


def back_kernel(pair_ref, line_ref, plane_ref, own_ref, *refs):
    flows, (part_ref, dist_ref, proj_ref, push_ref, place_ref) = refs[: len(CHUNKS)], refs[len(CHUNKS) :]
    lane = lax.broadcasted_iota(jnp.int32, (8, 128), 1)
    row = lax.broadcasted_iota(jnp.int32, (8, 128), 0)
    sources = [
        jnp.where(lane < 64, plane_ref[2 * i], pltpu.roll(plane_ref[2 * i + 1], 64, 1))
        for i in range(N_PLANE // 2)
    ]
    sources = jnp.concatenate(sources, axis=1)
    dist_ref[...], proj_ref[...], push_ref[...], place_ref[...] = source_features(
        pltpu.roll(sources, 5, 0), sources
    )
    own = pltpu.roll(own_ref[0], 3, 0)
    pieces = []
    for src in range(4):
        piece = pltpu.roll(own, 128 - 16 * src, 1) if src else own
        pieces.append(jnp.where((row >= 3) & (lane < 16), piece, 0.0))
    index = 0
    for flow_ref in flows:
        done, count = 0, flow_ref.shape[0]
        while done < count:
            wide = min(4, count - done)
            flow = pair_sums(
                side_by_side(line_ref, index, wide),
                BACK_SOURCES,
                dist_ref,
                proj_ref,
                push_ref,
                place_ref,
                4,
                0,
            )
            for i in range(wide):
                mine = (pair_ref[0] == index // 4).astype(F32)
                total = flow[:, 128 * i : 128 * i + 128] + flow_ref[done + i]
                part_ref[index] = jnp.where(row < 3, total, mine * pieces[index % 4])
                index += 1
            done += wide


def velocity_kernel(parts_ref, out_ref, density_ref):
    total = total_of(parts_ref)
    out_ref[:, 0, :] = total[0:3, 0:64]
    out_ref[:, 1, :] = total[0:3, 64:128]
    density_ref[:, 0, :] = total[3:6, 0:16]


def tiles(count):
    return jax.ShapeDtypeStruct((count, 8, 128), F32)


def cost(pairs):
    return pl.CostEstimate(flops=pairs * 400, bytes_accessed=1 << 20, transcendentals=pairs)


def params(mib):
    return pltpu.CompilerParams(vmem_limit_bytes=mib << 20)


def feature_shapes(count):
    return [((32, count), BF16), ((32, count), BF16), ((16, count), BF16), ((16, count), BF16)]


def exchange(x, axes):
    return lax.all_to_all(x, axes, 0, 0, tiled=True)


def per_device(fibre_points, shell_points, bending, shell_inverse):
    own_line, own_plane = pl.pallas_call(
        own_kernel, out_shape=[tiles(N_LINE), tiles(N_PLANE)], compiler_params=params(2)
    )(fibre_points, shell_points)
    plane = exchange(own_plane, PLANE)
    own_line, _ = lax.optimization_barrier((own_line, plane))
    features = [jax.ShapeDtypeStruct(s, t) for s, t in feature_shapes(SOURCES)]
    features = pl.pallas_call(
        source_kernel,
        out_shape=features,
        compiler_params=params(24),
        cost_estimate=cost(64 * SOURCES),
    )(plane, bending)
    line, features = lax.optimization_barrier((exchange(own_line, LINE), features))
    shell_part, shell_places = pl.pallas_call(
        shell_kernel,
        out_shape=[tiles(N_LINE), jax.ShapeDtypeStruct((8, 256), F32)],
        compiler_params=params(24),
        cost_estimate=cost(256 * SOURCES),
    )(line, *features)

    def fibre_chunk(chunk, after):
        held, _ = lax.optimization_barrier((line, after))
        first, widths = CHUNKS[chunk]
        return pl.pallas_call(
            functools.partial(fibre_kernel, first, widths),
            out_shape=tiles(sum(widths) // 128),
            compiler_params=params(24),
            cost_estimate=cost(sum(widths) * SOURCES),
        )(held, *features)

    flows = []

    def exchange_beside(x, axes):
        flow = fibre_chunk(len(flows), x)
        x, flow = lax.optimization_barrier((exchange(x, axes), flow))
        flows.append(flow)
        return x

    shell_parts = exchange_beside(shell_part, LINE)
    shell_own = pl.pallas_call(
        columns_kernel,
        out_shape=jax.ShapeDtypeStruct((N_PLANE, 16, 128), BF16),
        compiler_params=params(2),
    )(shell_parts)
    shell_all = exchange_beside(shell_own, PLANE)
    columns = shell_all[:, :3, :64].reshape(N_PLANE, 3, 4, 16)
    columns = columns.transpose(1, 3, 0, 2).reshape(3, 16, 128)
    density_rows = -jnp.einsum(
        "xaqcbn,cbn->xaq", shell_inverse, columns, preferred_element_type=F32
    )
    pair = lax.axis_index("tgt_2") * 2 + lax.axis_index("tgt_3")
    pair = pair.astype(jnp.int32).reshape(1)
    scalar = pl.BlockSpec(memory_space=pltpu.SMEM)
    vector = pl.BlockSpec(memory_space=pltpu.VMEM)
    density_own = pl.pallas_call(
        density_kernel,
        out_shape=tiles(N_PLANE),
        in_specs=[scalar, vector, vector],
        compiler_params=params(2),
    )(pair, density_rows, shell_places)
    density_all = exchange_beside(density_own, PLANE)
    part = pl.pallas_call(
        back_kernel,
        out_shape=tiles(N_LINE),
        grid=(1,),
        in_specs=[
            scalar,
            pl.BlockSpec((N_LINE, 8, 128), lambda i: (0, 0, 0)),
            pl.BlockSpec((N_PLANE, 8, 128), lambda i: (0, 0, 0)),
            pl.BlockSpec((1, 8, 128), lambda i: (0, 0, 0)),
        ]
        + [pl.BlockSpec(flow.shape, lambda i: (0, 0, 0)) for flow in flows],
        out_specs=pl.BlockSpec((N_LINE, 8, 128), lambda i: (0, 0, 0)),
        scratch_shapes=[pltpu.VMEM(s, t) for s, t in feature_shapes(BACK_SOURCES)],
        compiler_params=params(24),
        cost_estimate=cost(N_LINE * 128 * BACK_SOURCES),
    )(pair, line, density_all, density_own, *flows)
    velocity, density = pl.pallas_call(
        velocity_kernel,
        out_shape=[
            jax.ShapeDtypeStruct((3, 2, 64), F32),
            jax.ShapeDtypeStruct((3, 1, 16), F32),
        ],
        compiler_params=params(2),
    )(exchange(part, LINE))
    return velocity, density


def solution(mesh):
    torus = Mesh(mesh.devices.reshape(4, 8, 2, 2, mesh.shape["src"]), AXES)
    in_specs = (P(None, AXES, None), P(None, TGT, "src"), P(), P(None, TGT, None, None, "src", None))
    out_specs = (P(None, AXES, None), P(None, TGT, "src"))
    return jax.shard_map(per_device, mesh=torus, in_specs=in_specs, out_specs=out_specs, check_vma=False)
```

```python
import functools
import math

import jax
import jax.numpy as jnp
from jax import lax
from jax.experimental import pallas as pl
from jax.experimental.pallas import tpu as pltpu
from jax.sharding import Mesh
from jax.sharding import PartitionSpec as P

AXES = ("tgt_0", "tgt_1", "tgt_2", "tgt_3", "src")
TGT = AXES[:4]
LINE = ("tgt_2", "tgt_3", "src")
PLANE = ("tgt_0", "tgt_1")
N_LINE = 16
N_PLANE = 32
SOURCES = N_PLANE * 128
BACK_SOURCES = N_PLANE * 64
CHUNKS = ((0, (512,)), (4, (768,)), (10, (768,)))
STEP = 512
ROWS = (((0,), (0,)), ((), ()))

F32 = jnp.float32
BF16 = jnp.bfloat16
scale = 20.0
mobility = scale / (8.0 * math.pi)


def three_parts(x):
    high = x.astype(BF16).astype(F32)
    rest = x - high
    middle = rest.astype(BF16).astype(F32)
    low = (rest - middle).astype(BF16).astype(F32)
    return high, middle, low


def rows_of(x):
    return lax.broadcasted_iota(jnp.int32, x.shape, 0)


def left_rows(x, level):
    row = rows_of(x)
    a, b, c = three_parts(x)
    p, q, r = three_parts(level)
    first = jnp.where(row < 3, a, jnp.where(row == 3, p, jnp.where(row == 4, q, jnp.where(row == 5, r, 1.0))))
    second = jnp.where(row < 3, a, jnp.where(row == 3, 1.0, pltpu.roll(b, 4, 0)))
    return jnp.concatenate([first, second, b + pltpu.roll(a, 4, 0), c], axis=0).astype(BF16)


def right_rows(x, ones, level):
    row = rows_of(x)
    a, b, c = three_parts(x)
    p, q, r = three_parts(level)
    first = jnp.where(row < 3, a, jnp.where(row < 6, ones, jnp.where(row == 6, p, q)))
    second = jnp.where(row < 3, b, jnp.where(row == 3, r, pltpu.roll(a, 4, 0)))
    return jnp.concatenate([first, second, b + pltpu.roll(c, 4, 0), a], axis=0).astype(BF16)


def source_features(places, pushes):
    row = rows_of(places)
    places = jnp.where(row < 3, places * scale, 0.0)
    pushes = jnp.where(row < 3, pushes, 0.0)
    square = jnp.sum(places * places, axis=0, keepdims=True)
    along = jnp.sum(places * pushes, axis=0, keepdims=True)
    a, b, _ = three_parts(pushes)
    push_rows = jnp.concatenate([a, b], axis=0).astype(BF16)
    a, b, c = three_parts(jnp.where(row == 3, 1.0, places))
    place_rows = jnp.concatenate([a, b + pltpu.roll(c, 4, 0)], axis=0).astype(BF16)
    return right_rows(-2.0 * places, 1.0, square), right_rows(pushes, 0.0, -along), push_rows, place_rows


def pair_sums(targets, count, dist_ref, proj_ref, push_ref, place_ref, unroll, level):
    row = rows_of(targets)
    x = jnp.where(row < 3, targets * scale, 0.0)
    square = jnp.sum(x * x, axis=0, keepdims=True) + 1.0
    features = left_rows(x, square)
    width = features.shape[1]
    step = min(STEP, count)

    def add_block(k, sums):
        diag_sum, proj_sum = sums
        part = pl.ds(pl.multiple_of(k * step, step), step)
        dist_sq = lax.dot_general(dist_ref[:, part], features, ROWS, preferred_element_type=F32)
        along = lax.dot_general(proj_ref[:, part], features, ROWS, preferred_element_type=F32)
        inv_root = lax.rsqrt(dist_sq)
        inv_cubed = inv_root * inv_root * inv_root
        diag = inv_root + inv_cubed
        high = diag.astype(BF16)
        diag_sum += jnp.dot(push_ref[:, part], high, preferred_element_type=F32)
        if level > 0:
            low = (diag - high.astype(F32)).astype(BF16)
            diag_sum += jnp.dot(push_ref[:, part], low, preferred_element_type=F32)
        proj = along * inv_cubed
        high = proj.astype(BF16)
        proj_sum += jnp.dot(place_ref[:, part], high, preferred_element_type=F32)
        if level > 1:
            low = (proj - high.astype(F32)).astype(BF16)
            proj_sum += jnp.dot(place_ref[:, part], low, preferred_element_type=F32)
        return diag_sum, proj_sum

    start = (jnp.zeros((16, width), F32), jnp.zeros((16, width), F32))
    diag_sum, proj_sum = lax.fori_loop(0, count // step, add_block, start, unroll=unroll)
    rest = proj_sum[8:16]
    moved = proj_sum[0:8] + rest + pltpu.roll(rest, 4, 0)
    return (diag_sum[0:8] + diag_sum[8:16] + x * moved[3:4] - moved) * mobility


def side_by_side(ref, first, count):
    return jnp.concatenate([ref[first + i] for i in range(count)], axis=1)


def packed(tiles, first_row):
    row = rows_of(tiles[0])
    lane = lax.broadcasted_iota(jnp.int32, tiles[0].shape, 1)
    keep = (row >= first_row) & (row < first_row + 3) & (lane < 16)
    blocks = []
    for start in range(0, len(tiles), 8):
        block = jnp.zeros_like(tiles[0])
        for i, tile in enumerate(tiles[start : start + 8]):
            piece = jnp.where(keep, tile, 0.0)
            block += pltpu.roll(piece, 16 * i, 1) if i else piece
        blocks.append(pltpu.roll(block, 8 - first_row, 0) if first_row else block)
    return jnp.concatenate(blocks, axis=1)


def own_kernel(fibre_ref, shell_ref, line_ref, plane_ref):
    fibre = jnp.concatenate([fibre_ref[:, 0, :], fibre_ref[:, 1, :]], axis=1)
    shell = jnp.concatenate([shell_ref[:, 0, :], jnp.zeros((3, 112), F32)], axis=1)
    tile = jnp.concatenate([fibre, shell, jnp.zeros((2, 128), F32)], axis=0)
    line_ref[...] = jnp.broadcast_to(tile[None], line_ref.shape)
    plane_ref[...] = jnp.broadcast_to(tile[None], plane_ref.shape)


def source_kernel(plane_ref, bending_ref, dist_ref, proj_ref, push_ref, place_ref):
    square = bending_ref[...]
    zero = jnp.zeros_like(square)
    both = jnp.concatenate(
        [jnp.concatenate([square, zero], axis=1), jnp.concatenate([zero, square], axis=1)], axis=0
    )
    places = plane_ref[...].reshape(N_PLANE * 8, 128)
    pushes = -lax.dot_general(
        places, both, (((1,), (1,)), ((), ())), precision=lax.Precision.HIGHEST, preferred_element_type=F32
    )
    pushes = jnp.concatenate([pushes[8 * i : 8 * i + 8] for i in range(N_PLANE)], axis=1)
    places = side_by_side(plane_ref, 0, N_PLANE)
    dist_ref[...], proj_ref[...], push_ref[...], place_ref[...] = source_features(places, pushes)


def shell_kernel(line_ref, dist_ref, proj_ref, push_ref, place_ref, part_ref, shell_ref):
    shell_ref[...] = packed([line_ref[i] for i in range(N_LINE)], 3)
    order = [pair * 4 + src for src in range(4) for pair in range(4)]
    targets = packed([line_ref[i] for i in order], 3)
    flow = pair_sums(targets, SOURCES, dist_ref, proj_ref, push_ref, place_ref, 4, 2)
    for src in range(4):
        half = flow[:, 128 * (src // 2) : 128 * (src // 2) + 128]
        piece = pltpu.roll(half, 64, 1) if src % 2 else half
        for pair in range(4):
            part_ref[pair * 4 + src] = piece


def fibre_kernel(first, widths, line_ref, dist_ref, proj_ref, push_ref, place_ref, flow_ref):
    done = 0
    for width in widths:
        count = width // 128
        flow = pair_sums(
            side_by_side(line_ref, first + done, count),
            SOURCES,
            dist_ref,
            proj_ref,
            push_ref,
            place_ref,
            4,
            0,
        )
        for i in range(count):
            flow_ref[done + i] = flow[:, 128 * i : 128 * i + 128]
        done += count


def total_of(parts_ref):
    total = parts_ref[0]
    for i in range(1, parts_ref.shape[0]):
        total += parts_ref[i]
    return total


def columns_kernel(parts_ref, out_ref):
    total = total_of(parts_ref)
    total = total.astype(BF16).astype(F32)
    out_ref[...] = jnp.broadcast_to(total[None], out_ref.shape)


def density_kernel(pair_ref, columns_ref, inverse_ref, shell_ref, out_ref):
    columns = jnp.concatenate([columns_ref[:, c, :] for c in range(3)], axis=1).astype(BF16)
    here = lax.broadcasted_iota(jnp.int32, (N_PLANE, 512), 0)
    there = lax.broadcasted_iota(jnp.int32, (N_PLANE, 512), 1)
    pick = (there % 128 == 4 * here + there // 128).astype(F32).astype(BF16)
    spread = lax.dot_general(columns, pick, ROWS, preferred_element_type=F32)
    parts = []
    for c in range(3):
        part = jnp.zeros((16, 128), F32)
        for pair in range(4):
            first = 128 * c + 16 * pair
            part += spread[first : first + 16, 128 * pair : 128 * pair + 128]
        parts.append(part)
    ones = jnp.ones((8, 128), F32)
    row = lax.broadcasted_iota(jnp.int32, (8, 64), 0)
    density = jnp.zeros((8, 64), F32)
    for x in range(3):
        total = jnp.zeros((64, 8, 128), F32)
        for c in range(3):
            block = inverse_ref[x, 0, :, c].astype(F32) * parts[c][None]
            total += block[:, 0:8] + block[:, 8:16]
        sums = jnp.sum(total, axis=1)
        line = lax.dot_general(
            ones, sums, (((1,), (1,)), ((), ())), precision=lax.Precision.HIGHEST, preferred_element_type=F32
        )
        density -= jnp.where(row == x, line, 0.0)
    density = jnp.concatenate([density, jnp.zeros((8, 64), F32)], axis=1)
    lane = lax.broadcasted_iota(jnp.int32, density.shape, 1)
    places = jnp.zeros_like(density)
    for pair in range(4):
        half = shell_ref[:, 128 * (pair // 2) : 128 * (pair // 2) + 128]
        half = pltpu.roll(half, 64, 1) if pair % 2 else half
        places += jnp.where((pair_ref[0] == pair) & (lane < 64), half, 0.0)
    tile = density + pltpu.roll(places, 3, 0)
    out_ref[...] = jnp.broadcast_to(tile[None], out_ref.shape)


def back_kernel(pair_ref, line_ref, plane_ref, own_ref, *refs):
    flows, (part_ref, dist_ref, proj_ref, push_ref, place_ref) = refs[: len(CHUNKS)], refs[len(CHUNKS) :]
    lane = lax.broadcasted_iota(jnp.int32, (8, 128), 1)
    row = lax.broadcasted_iota(jnp.int32, (8, 128), 0)
    sources = [
        jnp.where(lane < 64, plane_ref[2 * i], pltpu.roll(plane_ref[2 * i + 1], 64, 1))
        for i in range(N_PLANE // 2)
    ]
    sources = jnp.concatenate(sources, axis=1)
    dist_ref[...], proj_ref[...], push_ref[...], place_ref[...] = source_features(
        pltpu.roll(sources, 5, 0), sources
    )
    own = pltpu.roll(own_ref[0], 3, 0)
    pieces = []
    for src in range(4):
        piece = pltpu.roll(own, 128 - 16 * src, 1) if src else own
        pieces.append(jnp.where((row >= 3) & (lane < 16), piece, 0.0))
    index = 0
    for flow_ref in flows:
        done, count = 0, flow_ref.shape[0]
        while done < count:
            wide = 6 if count % 6 == 0 else 4
            flow = pair_sums(
                side_by_side(line_ref, index, wide),
                BACK_SOURCES,
                dist_ref,
                proj_ref,
                push_ref,
                place_ref,
                4,
                0,
            )
            for i in range(wide):
                mine = (pair_ref[0] == index // 4).astype(F32)
                total = flow[:, 128 * i : 128 * i + 128] + flow_ref[done + i]
                part_ref[index] = jnp.where(row < 3, total, mine * pieces[index % 4])
                index += 1
            done += wide


def velocity_kernel(parts_ref, out_ref, density_ref):
    total = total_of(parts_ref)
    out_ref[:, 0, :] = total[0:3, 0:64]
    out_ref[:, 1, :] = total[0:3, 64:128]
    density_ref[:, 0, :] = total[3:6, 0:16]


def tiles(count):
    return jax.ShapeDtypeStruct((count, 8, 128), F32)


def cost(pairs):
    return pl.CostEstimate(flops=pairs * 400, bytes_accessed=1 << 20, transcendentals=pairs)


def params(mib):
    return pltpu.CompilerParams(vmem_limit_bytes=mib << 20)


def feature_shapes(count):
    return [((32, count), BF16), ((32, count), BF16), ((16, count), BF16), ((16, count), BF16)]


def exchange(x, axes):
    return lax.all_to_all(x, axes, 0, 0, tiled=True)


def per_device(fibre_points, shell_points, bending, shell_inverse):
    own_line, own_plane = pl.pallas_call(
        own_kernel, out_shape=[tiles(N_LINE), tiles(N_PLANE)], compiler_params=params(62)
    )(fibre_points, shell_points)
    plane = exchange(own_plane, PLANE)
    own_line, _ = lax.optimization_barrier((own_line, plane))
    features = [jax.ShapeDtypeStruct(s, t) for s, t in feature_shapes(SOURCES)]
    features = pl.pallas_call(
        source_kernel,
        out_shape=features,
        compiler_params=params(24),
        cost_estimate=cost(64 * SOURCES),
    )(plane, bending)
    line, features = lax.optimization_barrier((exchange(own_line, LINE), features))
    shell_part, shell_places = pl.pallas_call(
        shell_kernel,
        out_shape=[tiles(N_LINE), jax.ShapeDtypeStruct((8, 256), F32)],
        compiler_params=params(24),
        cost_estimate=cost(256 * SOURCES),
    )(line, *features)

    def fibre_chunk(chunk, after):
        held, _ = lax.optimization_barrier((line, after))
        first, widths = CHUNKS[chunk]
        return pl.pallas_call(
            functools.partial(fibre_kernel, first, widths),
            out_shape=tiles(sum(widths) // 128),
            compiler_params=params(24),
            cost_estimate=cost(sum(widths) * SOURCES),
        )(held, *features)

    flows = []

    def exchange_beside(x, axes):
        flow = fibre_chunk(len(flows), x)
        x, flow = lax.optimization_barrier((exchange(x, axes), flow))
        flows.append(flow)
        return x

    shell_parts = exchange_beside(shell_part, LINE)
    shell_own = pl.pallas_call(
        columns_kernel,
        out_shape=tiles(N_PLANE),
        compiler_params=params(2),
    )(shell_parts)
    shell_all = exchange_beside(shell_own, PLANE)
    pair = lax.axis_index("tgt_2") * 2 + lax.axis_index("tgt_3")
    pair = pair.astype(jnp.int32).reshape(1)
    scalar = pl.BlockSpec(memory_space=pltpu.SMEM)
    vector = pl.BlockSpec(memory_space=pltpu.VMEM)
    density_own = pl.pallas_call(
        density_kernel,
        out_shape=tiles(N_PLANE),
        in_specs=[scalar, vector, vector, vector],
        compiler_params=params(12),
    )(pair, shell_all, shell_inverse, shell_places)
    density_all = exchange_beside(density_own, PLANE)
    part = pl.pallas_call(
        back_kernel,
        out_shape=tiles(N_LINE),
        grid=(1,),
        in_specs=[
            scalar,
            pl.BlockSpec((N_LINE, 8, 128), lambda i: (0, 0, 0)),
            pl.BlockSpec((N_PLANE, 8, 128), lambda i: (0, 0, 0)),
            pl.BlockSpec((1, 8, 128), lambda i: (0, 0, 0)),
        ]
        + [pl.BlockSpec(flow.shape, lambda i: (0, 0, 0)) for flow in flows],
        out_specs=pl.BlockSpec((N_LINE, 8, 128), lambda i: (0, 0, 0)),
        scratch_shapes=[pltpu.VMEM(s, t) for s, t in feature_shapes(BACK_SOURCES)],
        compiler_params=params(24),
        cost_estimate=cost(N_LINE * 128 * BACK_SOURCES),
    )(pair, line, density_all, density_own, *flows)
    velocity, density = pl.pallas_call(
        velocity_kernel,
        out_shape=[
            jax.ShapeDtypeStruct((3, 2, 64), F32),
            jax.ShapeDtypeStruct((3, 1, 16), F32),
        ],
        compiler_params=params(2),
    )(exchange(part, LINE))
    return velocity, density


def solution(mesh):
    torus = Mesh(mesh.devices.reshape(4, 8, 2, 2, mesh.shape["src"]), AXES)
    in_specs = (P(None, AXES, None), P(None, TGT, "src"), P(), P(None, TGT, None, None, "src", None))
    out_specs = (P(None, AXES, None), P(None, TGT, "src"))
    return jax.shard_map(per_device, mesh=torus, in_specs=in_specs, out_specs=out_specs, check_vma=False)
```

```python
import functools
import math

import jax
import jax.numpy as jnp
from jax import lax
from jax.experimental import pallas as pl
from jax.experimental.pallas import tpu as pltpu
from jax.sharding import Mesh
from jax.sharding import PartitionSpec as P

AXES = ("tgt_0", "tgt_1", "tgt_2", "tgt_3", "src")
TGT = AXES[:4]
LINE = ("tgt_2", "tgt_3", "src")
PLANE = ("tgt_0", "tgt_1")
N_LINE = 16
N_PLANE = 32
SOURCES = N_PLANE * 128
BACK_SOURCES = N_PLANE * 64
CHUNKS = ((0, (512, 512)), (8, (512, 512)))
ROWS = (((0,), (0,)), ((), ()))

F32 = jnp.float32
BF16 = jnp.bfloat16
scale = 20.0
mobility = scale / (8.0 * math.pi)


def three_parts(x):
    high = x.astype(BF16).astype(F32)
    rest = x - high
    middle = rest.astype(BF16).astype(F32)
    low = (rest - middle).astype(BF16).astype(F32)
    return high, middle, low


def rows_of(x):
    return lax.broadcasted_iota(jnp.int32, x.shape, 0)


def left_rows(x, level):
    row = rows_of(x)
    a, b, c = three_parts(x)
    p, q, r = three_parts(level)
    first = jnp.where(row < 3, a, jnp.where(row == 3, p, jnp.where(row == 4, q, jnp.where(row == 5, r, 1.0))))
    second = jnp.where(row < 3, a, jnp.where(row == 3, 1.0, pltpu.roll(b, 4, 0)))
    return jnp.concatenate([first, second, b + pltpu.roll(a, 4, 0), c], axis=0).astype(BF16)


def right_rows(x, ones, level):
    row = rows_of(x)
    a, b, c = three_parts(x)
    p, q, r = three_parts(level)
    first = jnp.where(row < 3, a, jnp.where(row < 6, ones, jnp.where(row == 6, p, q)))
    second = jnp.where(row < 3, b, jnp.where(row == 3, r, pltpu.roll(a, 4, 0)))
    return jnp.concatenate([first, second, b + pltpu.roll(c, 4, 0), a], axis=0).astype(BF16)


def source_features(places, pushes):
    row = rows_of(places)
    center = jnp.mean(places, axis=1, keepdims=True)
    places = jnp.where(row < 3, (places - center) * scale, 0.0)
    pushes = jnp.where(row < 3, pushes, 0.0)
    square = jnp.sum(places * places, axis=0, keepdims=True)
    along = jnp.sum(places * pushes, axis=0, keepdims=True)
    a, b, _ = three_parts(pushes)
    push_rows = jnp.concatenate([a, b], axis=0).astype(BF16)
    y, g = places[0:3], pushes[0:3]
    form = jnp.concatenate(
        [g, along, along * y, g[2:3] * y[2:3], g[0:1] * y, g[1:2] * y, g[2:3] * y[0:2]], axis=0
    )
    form_rows = jnp.concatenate(three_parts(form), axis=0).astype(BF16)
    center = jnp.broadcast_to(center, (8, 128))
    return right_rows(-2.0 * places, 1.0, square), push_rows, form_rows, center


def pair_sums(targets, count, dist_ref, push_ref, form_ref, center_ref, step, unroll, fine):
    row = rows_of(targets)
    x = jnp.where(row < 3, (targets - center_ref[:, 0:1]) * scale, 0.0)
    square = jnp.sum(x * x, axis=0, keepdims=True) + 1.0
    features = left_rows(x, square)
    width = features.shape[1]

    def add_block(k, sums):
        root_sum, cube_sum = sums
        part = pl.ds(pl.multiple_of(k * step, step), step)
        dist_sq = lax.dot_general(dist_ref[:, part], features, ROWS, preferred_element_type=F32)
        root = lax.rsqrt(dist_sq)
        high = root.astype(BF16)
        root_sum += jnp.dot(push_ref[:, part], high, preferred_element_type=F32)
        if fine:
            low = (root - high.astype(F32)).astype(BF16)
            root_sum += jnp.dot(push_ref[:, part], low, preferred_element_type=F32)
        cube = root * root * root
        high = cube.astype(BF16)
        cube_sum += jnp.dot(form_ref[:, part], high, preferred_element_type=F32)
        if fine:
            low = (cube - high.astype(F32)).astype(BF16)
            cube_sum += jnp.dot(form_ref[:, part], low, preferred_element_type=F32)
        return root_sum, cube_sum

    start = (jnp.zeros((16, width), F32), jnp.zeros((48, width), F32))
    root_sum, cube_sum = lax.fori_loop(0, count // step, add_block, start, unroll=unroll)
    form = cube_sum[0:16] + cube_sum[16:32] + cube_sum[32:48]
    x0, x1, x2 = x[0:1], x[1:2], x[2:3]
    pull = x0 * form[0:1] + x1 * form[1:2] + x2 * form[2:3] - form[3:4]
    last = jnp.concatenate([form[14:16], form[7:8]], axis=0)
    moved = x0 * form[8:11] + x1 * form[11:14] + x2 * last - form[4:7]
    flow = root_sum[0:3] + root_sum[8:11] + form[0:3] + (x[0:3] * pull - moved)
    return jnp.concatenate([flow * mobility, jnp.zeros((5, width), F32)], axis=0)


def side_by_side(ref, first, count):
    return jnp.concatenate([ref[first + i] for i in range(count)], axis=1)


def packed(tiles, first_row):
    row = rows_of(tiles[0])
    lane = lax.broadcasted_iota(jnp.int32, tiles[0].shape, 1)
    keep = (row >= first_row) & (row < first_row + 3) & (lane < 16)
    blocks = []
    for start in range(0, len(tiles), 8):
        block = jnp.zeros_like(tiles[0])
        for i, tile in enumerate(tiles[start : start + 8]):
            piece = jnp.where(keep, tile, 0.0)
            block += pltpu.roll(piece, 16 * i, 1) if i else piece
        blocks.append(pltpu.roll(block, 8 - first_row, 0) if first_row else block)
    return jnp.concatenate(blocks, axis=1)


def own_kernel(fibre_ref, shell_ref, line_ref, plane_ref):
    fibre = jnp.concatenate([fibre_ref[:, 0, :], fibre_ref[:, 1, :]], axis=1)
    shell = jnp.concatenate([shell_ref[:, 0, :], jnp.zeros((3, 112), F32)], axis=1)
    tile = jnp.concatenate([fibre, shell, jnp.zeros((2, 128), F32)], axis=0)
    line_ref[...] = jnp.broadcast_to(tile[None], line_ref.shape)
    plane_ref[...] = jnp.broadcast_to(tile[None], plane_ref.shape)


def source_kernel(plane_ref, bending_ref, dist_ref, push_ref, form_ref, center_ref):
    square = bending_ref[...]
    zero = jnp.zeros_like(square)
    both = jnp.concatenate(
        [jnp.concatenate([square, zero], axis=1), jnp.concatenate([zero, square], axis=1)], axis=0
    )
    places = plane_ref[...].reshape(N_PLANE * 8, 128)
    pushes = -lax.dot_general(
        places, both, (((1,), (1,)), ((), ())), precision=lax.Precision.HIGHEST, preferred_element_type=F32
    )
    pushes = jnp.concatenate([pushes[8 * i : 8 * i + 8] for i in range(N_PLANE)], axis=1)
    places = side_by_side(plane_ref, 0, N_PLANE)
    dist_ref[...], push_ref[...], form_ref[...], center_ref[...] = source_features(places, pushes)


def shell_kernel(line_ref, dist_ref, push_ref, form_ref, center_ref, part_ref, shell_ref):
    shell_ref[...] = packed([line_ref[i] for i in range(N_LINE)], 3)
    order = [pair * 4 + src for src in range(4) for pair in range(4)]
    targets = packed([line_ref[i] for i in order], 3)
    flow = pair_sums(targets, SOURCES, dist_ref, push_ref, form_ref, center_ref, 1024, 4, True)
    for src in range(4):
        half = flow[:, 128 * (src // 2) : 128 * (src // 2) + 128]
        piece = pltpu.roll(half, 64, 1) if src % 2 else half
        for pair in range(4):
            part_ref[pair * 4 + src] = piece


def fibre_kernel(first, widths, line_ref, dist_ref, push_ref, form_ref, center_ref, flow_ref):
    done = 0
    for width in widths:
        count = width // 128
        flow = pair_sums(
            side_by_side(line_ref, first + done, count),
            SOURCES,
            dist_ref,
            push_ref,
            form_ref,
            center_ref,
            1024,
            4,
            False,
        )
        for i in range(count):
            flow_ref[done + i] = flow[:, 128 * i : 128 * i + 128]
        done += count


def total_of(parts_ref):
    total = parts_ref[0]
    for i in range(1, parts_ref.shape[0]):
        total += parts_ref[i]
    return total


def columns_kernel(parts_ref, out_ref):
    total = total_of(parts_ref)
    total = total.astype(BF16).astype(F32)
    out_ref[...] = jnp.broadcast_to(total[None], out_ref.shape)


def density_kernel(pair_ref, columns_ref, inverse_ref, shell_ref, out_ref):
    columns = jnp.concatenate([columns_ref[:, c, :] for c in range(3)], axis=1).astype(BF16)
    here = lax.broadcasted_iota(jnp.int32, (N_PLANE, 512), 0)
    there = lax.broadcasted_iota(jnp.int32, (N_PLANE, 512), 1)
    pick = (there % 128 == 4 * here + there // 128).astype(F32).astype(BF16)
    spread = lax.dot_general(columns, pick, ROWS, preferred_element_type=F32)
    parts = []
    for c in range(3):
        part = jnp.zeros((16, 128), F32)
        for pair in range(4):
            first = 128 * c + 16 * pair
            part += spread[first : first + 16, 128 * pair : 128 * pair + 128]
        parts.append(part)
    ones = jnp.ones((8, 128), F32)
    row = lax.broadcasted_iota(jnp.int32, (8, 64), 0)
    density = jnp.zeros((8, 64), F32)
    for x in range(3):
        total = jnp.zeros((64, 8, 128), F32)
        for c in range(3):
            block = inverse_ref[x, 0, :, c].astype(F32) * parts[c][None]
            total += block[:, 0:8] + block[:, 8:16]
        sums = jnp.sum(total, axis=1)
        line = lax.dot_general(
            ones, sums, (((1,), (1,)), ((), ())), precision=lax.Precision.HIGHEST, preferred_element_type=F32
        )
        density -= jnp.where(row == x, line, 0.0)
    density = jnp.concatenate([density, jnp.zeros((8, 64), F32)], axis=1)
    lane = lax.broadcasted_iota(jnp.int32, density.shape, 1)
    places = jnp.zeros_like(density)
    for pair in range(4):
        half = shell_ref[:, 128 * (pair // 2) : 128 * (pair // 2) + 128]
        half = pltpu.roll(half, 64, 1) if pair % 2 else half
        places += jnp.where((pair_ref[0] == pair) & (lane < 64), half, 0.0)
    tile = density + pltpu.roll(places, 3, 0)
    out_ref[...] = jnp.broadcast_to(tile[None], out_ref.shape)


def back_kernel(pair_ref, line_ref, plane_ref, own_ref, *refs):
    flows, (part_ref, dist_ref, push_ref, form_ref, center_ref) = refs[: len(CHUNKS)], refs[len(CHUNKS) :]
    lane = lax.broadcasted_iota(jnp.int32, (8, 128), 1)
    row = lax.broadcasted_iota(jnp.int32, (8, 128), 0)
    sources = [
        jnp.where(lane < 64, plane_ref[2 * i], pltpu.roll(plane_ref[2 * i + 1], 64, 1))
        for i in range(N_PLANE // 2)
    ]
    sources = jnp.concatenate(sources, axis=1)
    dist_ref[...], push_ref[...], form_ref[...], center_ref[...] = source_features(
        pltpu.roll(sources, 5, 0), sources
    )
    own = pltpu.roll(own_ref[0], 3, 0)
    pieces = []
    for src in range(4):
        piece = pltpu.roll(own, 128 - 16 * src, 1) if src else own
        pieces.append(jnp.where((row >= 3) & (lane < 16), piece, 0.0))
    index = 0
    for flow_ref in flows:
        done, count = 0, flow_ref.shape[0]
        while done < count:
            wide = min(4, count - done)
            flow = pair_sums(
                side_by_side(line_ref, index, wide),
                BACK_SOURCES,
                dist_ref,
                push_ref,
                form_ref,
                center_ref,
                1024,
                2,
                False,
            )
            for i in range(wide):
                mine = (pair_ref[0] == index // 4).astype(F32)
                total = flow[:, 128 * i : 128 * i + 128] + flow_ref[done + i]
                part_ref[index] = jnp.where(row < 3, total, mine * pieces[index % 4])
                index += 1
            done += wide


def velocity_kernel(parts_ref, out_ref, density_ref):
    total = total_of(parts_ref)
    out_ref[:, 0, :] = total[0:3, 0:64]
    out_ref[:, 1, :] = total[0:3, 64:128]
    density_ref[:, 0, :] = total[3:6, 0:16]


def tiles(count):
    return jax.ShapeDtypeStruct((count, 8, 128), F32)


def cost(pairs):
    return pl.CostEstimate(flops=pairs * 400, bytes_accessed=1 << 20, transcendentals=pairs)


def params(mib):
    return pltpu.CompilerParams(vmem_limit_bytes=mib << 20)


def feature_shapes(count):
    return [((32, count), BF16), ((16, count), BF16), ((48, count), BF16), ((8, 128), F32)]


def exchange(x, axes):
    return lax.all_to_all(x, axes, 0, 0, tiled=True)


def per_device(fibre_points, shell_points, bending, shell_inverse):
    own_line, own_plane = pl.pallas_call(
        own_kernel, out_shape=[tiles(N_LINE), tiles(N_PLANE)], compiler_params=params(62)
    )(fibre_points, shell_points)
    plane = exchange(own_plane, PLANE)
    own_line, _ = lax.optimization_barrier((own_line, plane))
    features = [jax.ShapeDtypeStruct(s, t) for s, t in feature_shapes(SOURCES)]
    features = pl.pallas_call(
        source_kernel,
        out_shape=features,
        compiler_params=params(24),
        cost_estimate=cost(64 * SOURCES),
    )(plane, bending)
    line, features = lax.optimization_barrier((exchange(own_line, LINE), features))
    shell_part, shell_places = pl.pallas_call(
        shell_kernel,
        out_shape=[tiles(N_LINE), jax.ShapeDtypeStruct((8, 256), F32)],
        compiler_params=params(24),
        cost_estimate=cost(256 * SOURCES),
    )(line, *features)

    def fibre_chunk(chunk, after):
        held, _ = lax.optimization_barrier((line, after))
        first, widths = CHUNKS[chunk]
        return pl.pallas_call(
            functools.partial(fibre_kernel, first, widths),
            out_shape=tiles(sum(widths) // 128),
            compiler_params=params(24),
            cost_estimate=cost(sum(widths) * SOURCES),
        )(held, *features)

    flows = []

    def exchange_beside(x, axes):
        flow = fibre_chunk(len(flows), x)
        x, flow = lax.optimization_barrier((exchange(x, axes), flow))
        flows.append(flow)
        return x

    shell_parts = exchange(shell_part, LINE)
    shell_own = pl.pallas_call(
        columns_kernel,
        out_shape=tiles(N_PLANE),
        compiler_params=params(2),
    )(shell_parts)
    shell_all = exchange_beside(shell_own, PLANE)
    pair = lax.axis_index("tgt_2") * 2 + lax.axis_index("tgt_3")
    pair = pair.astype(jnp.int32).reshape(1)
    scalar = pl.BlockSpec(memory_space=pltpu.SMEM)
    vector = pl.BlockSpec(memory_space=pltpu.VMEM)
    density_own = pl.pallas_call(
        density_kernel,
        out_shape=tiles(N_PLANE),
        in_specs=[scalar, vector, vector, vector],
        compiler_params=params(12),
    )(pair, shell_all, shell_inverse, shell_places)
    density_all = exchange_beside(density_own, PLANE)
    part = pl.pallas_call(
        back_kernel,
        out_shape=tiles(N_LINE),
        grid=(1,),
        in_specs=[
            scalar,
            pl.BlockSpec((N_LINE, 8, 128), lambda i: (0, 0, 0)),
            pl.BlockSpec((N_PLANE, 8, 128), lambda i: (0, 0, 0)),
            pl.BlockSpec((1, 8, 128), lambda i: (0, 0, 0)),
        ]
        + [pl.BlockSpec(flow.shape, lambda i: (0, 0, 0)) for flow in flows],
        out_specs=pl.BlockSpec((N_LINE, 8, 128), lambda i: (0, 0, 0)),
        scratch_shapes=[pltpu.VMEM(s, t) for s, t in feature_shapes(BACK_SOURCES)],
        compiler_params=params(24),
        cost_estimate=cost(N_LINE * 128 * BACK_SOURCES),
    )(pair, line, density_all, density_own, *flows)
    velocity, density = pl.pallas_call(
        velocity_kernel,
        out_shape=[
            jax.ShapeDtypeStruct((3, 2, 64), F32),
            jax.ShapeDtypeStruct((3, 1, 16), F32),
        ],
        compiler_params=params(2),
    )(exchange(part, LINE))
    return velocity, density


def solution(mesh):
    torus = Mesh(mesh.devices.reshape(4, 8, 2, 2, mesh.shape["src"]), AXES)
    in_specs = (P(None, AXES, None), P(None, TGT, "src"), P(), P(None, TGT, None, None, "src", None))
    out_specs = (P(None, AXES, None), P(None, TGT, "src"))
    return jax.shard_map(per_device, mesh=torus, in_specs=in_specs, out_specs=out_specs, check_vma=False)
```

```python
import functools
import math

import jax
import jax.numpy as jnp
from jax import lax
from jax.experimental import pallas as pl
from jax.experimental.pallas import tpu as pltpu
from jax.sharding import Mesh
from jax.sharding import PartitionSpec as P

AXES = ("tgt_0", "tgt_1", "tgt_2", "tgt_3", "src")
TGT = AXES[:4]
LINE = ("tgt_2", "tgt_3", "src")
PLANE = ("tgt_0", "tgt_1")
N_LINE = 16
N_PLANE = 32
SOURCES = N_PLANE * 128
LINE_SOURCES = N_LINE * 128
CHUNKS = ((0, 1), (4, 5), (24, 2))
WIDE = 4
ROW_SOURCES = 256
ROWS = (((0,), (0,)), ((), ()))

F32 = jnp.float32
BF16 = jnp.bfloat16
scale = 20.0
mobility = scale / (8.0 * math.pi)


def three_parts(x):
    high = x.astype(BF16).astype(F32)
    rest = x - high
    middle = rest.astype(BF16).astype(F32)
    low = (rest - middle).astype(BF16).astype(F32)
    return high, middle, low


def rows_of(x):
    return lax.broadcasted_iota(jnp.int32, x.shape, 0)


def left_rows(x, level):
    row = rows_of(x)
    a, b, c = three_parts(x)
    p, q, r = three_parts(level)
    first = jnp.where(row < 3, a, jnp.where(row == 3, p, jnp.where(row == 4, q, jnp.where(row == 5, r, 1.0))))
    second = jnp.where(row < 3, a, jnp.where(row == 3, 1.0, pltpu.roll(b, 4, 0)))
    return jnp.concatenate([first, second, b + pltpu.roll(a, 4, 0), c], axis=0).astype(BF16)


def right_rows(x, ones, level):
    row = rows_of(x)
    a, b, c = three_parts(x)
    p, q, r = three_parts(level)
    first = jnp.where(row < 3, a, jnp.where(row < 6, ones, jnp.where(row == 6, p, q)))
    second = jnp.where(row < 3, b, jnp.where(row == 3, r, pltpu.roll(a, 4, 0)))
    return jnp.concatenate([first, second, b + pltpu.roll(c, 4, 0), a], axis=0).astype(BF16)


def source_features(places, pushes):
    row = rows_of(places)
    center = jnp.mean(places, axis=1, keepdims=True)
    places = jnp.where(row < 3, (places - center) * scale, 0.0)
    pushes = jnp.where(row < 3, pushes, 0.0)
    square = jnp.sum(places * places, axis=0, keepdims=True)
    along = jnp.sum(places * pushes, axis=0, keepdims=True)
    a, b, _ = three_parts(pushes)
    push_rows = jnp.concatenate([a, b], axis=0).astype(BF16)
    y, g = places[0:3], pushes[0:3]
    form = jnp.concatenate(
        [g, along, along * y, g[2:3] * y[2:3], g[0:1] * y, g[1:2] * y, g[2:3] * y[0:2]], axis=0
    )
    form_rows = jnp.concatenate(three_parts(form), axis=0).astype(BF16)
    center = jnp.broadcast_to(center, (8, 128))
    return right_rows(-2.0 * places, 1.0, square), push_rows, form_rows, center


def pair_sums(targets, count, dist_ref, push_ref, form_ref, center_ref, step, unroll, fine):
    row = rows_of(targets)
    x = jnp.where(row < 3, (targets - center_ref[:, 0:1]) * scale, 0.0)
    square = jnp.sum(x * x, axis=0, keepdims=True) + 1.0
    features = left_rows(x, square)
    width = features.shape[1]

    def add_block(k, sums):
        root_sum, cube_sum = sums
        part = pl.ds(pl.multiple_of(k * step, step), step)
        dist_sq = lax.dot_general(dist_ref[:, part], features, ROWS, preferred_element_type=F32)
        root = lax.rsqrt(dist_sq)
        high = root.astype(BF16)
        root_sum += jnp.dot(push_ref[:, part], high, preferred_element_type=F32)
        if fine:
            low = (root - high.astype(F32)).astype(BF16)
            root_sum += jnp.dot(push_ref[:, part], low, preferred_element_type=F32)
        cube = root * root * root
        high = cube.astype(BF16)
        cube_sum += jnp.dot(form_ref[:, part], high, preferred_element_type=F32)
        if fine:
            low = (cube - high.astype(F32)).astype(BF16)
            cube_sum += jnp.dot(form_ref[:, part], low, preferred_element_type=F32)
        return root_sum, cube_sum

    start = (jnp.zeros((16, width), F32), jnp.zeros((48, width), F32))
    root_sum, cube_sum = lax.fori_loop(0, count // step, add_block, start, unroll=unroll)
    form = cube_sum[0:16] + cube_sum[16:32] + cube_sum[32:48]
    x0, x1, x2 = x[0:1], x[1:2], x[2:3]
    pull = x0 * form[0:1] + x1 * form[1:2] + x2 * form[2:3] - form[3:4]
    last = jnp.concatenate([form[14:16], form[7:8]], axis=0)
    moved = x0 * form[8:11] + x1 * form[11:14] + x2 * last - form[4:7]
    flow = root_sum[0:3] + root_sum[8:11] + form[0:3] + (x[0:3] * pull - moved)
    return jnp.concatenate([flow * mobility, jnp.zeros((5, width), F32)], axis=0)


def side_by_side(ref, first, count):
    return jnp.concatenate([ref[first + i] for i in range(count)], axis=1)


def packed(tiles, first_row):
    row = rows_of(tiles[0])
    lane = lax.broadcasted_iota(jnp.int32, tiles[0].shape, 1)
    keep = (row >= first_row) & (row < first_row + 3) & (lane < 16)
    blocks = []
    for start in range(0, len(tiles), 8):
        block = jnp.zeros_like(tiles[0])
        for i, tile in enumerate(tiles[start : start + 8]):
            piece = jnp.where(keep, tile, 0.0)
            block += pltpu.roll(piece, 16 * i, 1) if i else piece
        blocks.append(pltpu.roll(block, 8 - first_row, 0) if first_row else block)
    return jnp.concatenate(blocks, axis=1)


def own_kernel(fibre_ref, shell_ref, line_ref, plane_ref):
    fibre = jnp.concatenate([fibre_ref[:, 0, :], fibre_ref[:, 1, :]], axis=1)
    shell = jnp.concatenate([shell_ref[:, 0, :], jnp.zeros((3, 112), F32)], axis=1)
    tile = jnp.concatenate([fibre, shell, jnp.zeros((2, 128), F32)], axis=0)
    line_ref[...] = jnp.broadcast_to(tile[None], line_ref.shape)
    plane_ref[...] = jnp.broadcast_to(tile[None], plane_ref.shape)


def source_kernel(tiles_ref, bending_ref, dist_ref, push_ref, form_ref, center_ref):
    count = tiles_ref.shape[0]
    square = bending_ref[...]
    zero = jnp.zeros_like(square)
    both = jnp.concatenate(
        [jnp.concatenate([square, zero], axis=1), jnp.concatenate([zero, square], axis=1)], axis=0
    )
    pushes = -lax.dot_general(
        tiles_ref[...].reshape(count * 8, 128),
        both,
        (((1,), (1,)), ((), ())),
        precision=lax.Precision.HIGHEST,
        preferred_element_type=F32,
    )
    pushes = jnp.concatenate([pushes[8 * i : 8 * i + 8] for i in range(count)], axis=1)
    places = side_by_side(tiles_ref, 0, count)
    dist_ref[...], push_ref[...], form_ref[...], center_ref[...] = source_features(places, pushes)


def shell_kernel(line_ref, dist_ref, push_ref, form_ref, center_ref, part_ref, shell_ref):
    shell_ref[...] = packed([line_ref[i] for i in range(N_LINE)], 3)
    order = [pair * 4 + src for src in range(4) for pair in range(4)]
    targets = packed([line_ref[i] for i in order], 3)
    flow = pair_sums(targets, SOURCES, dist_ref, push_ref, form_ref, center_ref, 1024, 4, True)
    for src in range(4):
        half = flow[:, 128 * (src // 2) : 128 * (src // 2) + 128]
        piece = pltpu.roll(half, 64, 1) if src % 2 else half
        for pair in range(4):
            part_ref[pair * 4 + src] = piece


def fibre_kernel(first, parts, plane_ref, dist_ref, push_ref, form_ref, center_ref, flow_ref):
    for part in range(parts):
        flow = pair_sums(
            side_by_side(plane_ref, first + part * WIDE, WIDE),
            LINE_SOURCES,
            dist_ref,
            push_ref,
            form_ref,
            center_ref,
            1024,
            2,
            False,
        )
        for i in range(WIDE):
            flow_ref[part * WIDE + i] = flow[:, 128 * i : 128 * i + 128]


def total_of(parts_ref):
    total = parts_ref[0]
    for i in range(1, parts_ref.shape[0]):
        total += parts_ref[i]
    return total


def columns_kernel(parts_ref, out_ref):
    total = total_of(parts_ref)
    total = total.astype(BF16).astype(F32)
    out_ref[...] = jnp.broadcast_to(total[None], out_ref.shape)


def density_kernel(pair_ref, columns_ref, inverse_ref, out_ref):
    columns = jnp.concatenate([columns_ref[:, c, :] for c in range(3)], axis=1).astype(BF16)
    here = lax.broadcasted_iota(jnp.int32, (N_PLANE, 512), 0)
    there = lax.broadcasted_iota(jnp.int32, (N_PLANE, 512), 1)
    pick = (there % 128 == 4 * here + there // 128).astype(F32).astype(BF16)
    spread = lax.dot_general(columns, pick, ROWS, preferred_element_type=F32)
    parts = []
    for c in range(3):
        part = jnp.zeros((16, 128), F32)
        for pair in range(4):
            first = 128 * c + 16 * pair
            part += spread[first : first + 16, 128 * pair : 128 * pair + 128]
        parts.append(part)
    ones = jnp.ones((8, 128), F32)
    row = lax.broadcasted_iota(jnp.int32, (8, 64), 0)
    density = jnp.zeros((8, 64), F32)
    for x in range(3):
        total = jnp.zeros((64, 8, 128), F32)
        for c in range(3):
            block = inverse_ref[x, 0, :, c].astype(F32) * parts[c][None]
            total += block[:, 0:8] + block[:, 8:16]
        sums = jnp.sum(total, axis=1)
        line = lax.dot_general(
            ones, sums, (((1,), (1,)), ((), ())), precision=lax.Precision.HIGHEST, preferred_element_type=F32
        )
        density -= jnp.where(row == x, line, 0.0)
    density = jnp.concatenate([density, jnp.zeros((8, 64), F32)], axis=1)
    row = rows_of(density)
    lane = lax.broadcasted_iota(jnp.int32, density.shape, 1)
    lower = pltpu.roll(density, 3, 0)
    for src in range(4):
        piece = pltpu.roll(lower, 128 - 16 * src, 1) if src else lower
        piece = jnp.where((row >= 3) & (lane < 16), piece, 0.0)
        for pair in range(4):
            mine = (pair_ref[0] == pair).astype(F32)
            out_ref[pair * 4 + src] = density + mine * piece


def back_kernel(parts_ref, shell_ref, plane_ref, *refs):
    flows, refs = refs[: len(CHUNKS)], refs[len(CHUNKS) :]
    part_ref, density_ref, dist_ref, push_ref, form_ref, center_ref = refs
    lane = lax.broadcasted_iota(jnp.int32, (8, 128), 1)
    pairs = []
    for pair in range(4):
        total = parts_ref[pair * 4]
        for src in range(1, 4):
            total += parts_ref[pair * 4 + src]
        pairs.append(total)
    whole = (pairs[0] + pairs[1]) + (pairs[2] + pairs[3])
    density_ref[:, 0, :] = whole[3:6, 0:16]
    halves = [
        jnp.where(lane < 64, pairs[i], pltpu.roll(pairs[i + 1], 64, 1)) for i in (0, 2)
    ]
    dist_ref[...], push_ref[...], form_ref[...], center_ref[...] = source_features(
        shell_ref[...], jnp.concatenate(halves, axis=1)
    )
    for (first, parts), flow_ref in zip(CHUNKS, flows):
        for part in range(parts):
            index = first + part * WIDE
            flow = pair_sums(
                side_by_side(plane_ref, index, WIDE),
                ROW_SOURCES,
                dist_ref,
                push_ref,
                form_ref,
                center_ref,
                ROW_SOURCES,
                1,
                False,
            )
            for i in range(WIDE):
                part_ref[index + i] = flow[:, 128 * i : 128 * i + 128] + flow_ref[part * WIDE + i]


def velocity_kernel(parts_ref, out_ref):
    total = total_of(parts_ref)
    out_ref[:, 0, :] = total[0:3, 0:64]
    out_ref[:, 1, :] = total[0:3, 64:128]


def tiles(count):
    return jax.ShapeDtypeStruct((count, 8, 128), F32)


def cost(pairs):
    return pl.CostEstimate(flops=pairs * 400, bytes_accessed=1 << 20, transcendentals=pairs)


def params(mib):
    return pltpu.CompilerParams(vmem_limit_bytes=mib << 20)


def feature_shapes(count):
    return [((32, count), BF16), ((16, count), BF16), ((48, count), BF16), ((8, 128), F32)]


def exchange(x, axes):
    return lax.all_to_all(x, axes, 0, 0, tiled=True)


def per_device(fibre_points, shell_points, bending, shell_inverse):
    own_line, own_plane = pl.pallas_call(
        own_kernel, out_shape=[tiles(N_LINE), tiles(N_PLANE)], compiler_params=params(62)
    )(fibre_points, shell_points)
    plane = exchange(own_plane, PLANE)
    own_line, _ = lax.optimization_barrier((own_line, plane))

    def features_of(x):
        count = x.shape[0] * 128
        return pl.pallas_call(
            source_kernel,
            out_shape=[jax.ShapeDtypeStruct(s, t) for s, t in feature_shapes(count)],
            compiler_params=params(24),
            cost_estimate=cost(64 * count),
        )(x, bending)

    features = features_of(plane)
    line, features = lax.optimization_barrier((exchange(own_line, LINE), features))
    shell_part, shell_places = pl.pallas_call(
        shell_kernel,
        out_shape=[tiles(N_LINE), jax.ShapeDtypeStruct((8, 256), F32)],
        compiler_params=params(24),
        cost_estimate=cost(256 * SOURCES),
    )(line, *features)
    held, _ = lax.optimization_barrier((line, shell_part))
    features = features_of(held)
    flows = []

    def exchange_beside(x, axes):
        first, parts = CHUNKS[len(flows)]
        held, _ = lax.optimization_barrier((plane, x))
        flow = pl.pallas_call(
            functools.partial(fibre_kernel, first, parts),
            out_shape=tiles(parts * WIDE),
            compiler_params=params(24),
            cost_estimate=cost(parts * WIDE * 128 * LINE_SOURCES),
        )(held, *features)
        x, flow = lax.optimization_barrier((exchange(x, axes), flow))
        flows.append(flow)
        return x

    shell_own = pl.pallas_call(
        columns_kernel, out_shape=tiles(N_PLANE), compiler_params=params(2)
    )(exchange_beside(shell_part, LINE))
    shell_all = exchange_beside(shell_own, PLANE)
    pair = lax.axis_index("tgt_2") * 2 + lax.axis_index("tgt_3")
    message = pl.pallas_call(
        density_kernel,
        out_shape=tiles(N_LINE),
        in_specs=[pl.BlockSpec(memory_space=pltpu.SMEM)] + [pl.BlockSpec(memory_space=pltpu.VMEM)] * 2,
        compiler_params=params(12),
    )(pair.astype(jnp.int32).reshape(1), shell_all, shell_inverse)
    density_parts = exchange_beside(message, LINE)
    part, density = pl.pallas_call(
        back_kernel,
        out_shape=[tiles(N_PLANE), jax.ShapeDtypeStruct((3, 1, 16), F32)],
        scratch_shapes=[pltpu.VMEM(s, t) for s, t in feature_shapes(ROW_SOURCES)],
        compiler_params=params(24),
        cost_estimate=cost(ROW_SOURCES * SOURCES),
    )(density_parts, shell_places, plane, *flows)
    velocity = pl.pallas_call(
        velocity_kernel, out_shape=jax.ShapeDtypeStruct((3, 2, 64), F32), compiler_params=params(2)
    )(exchange(part, PLANE))
    return velocity, density


def solution(mesh):
    torus = Mesh(mesh.devices.reshape(4, 8, 2, 2, mesh.shape["src"]), AXES)
    in_specs = (P(None, AXES, None), P(None, TGT, "src"), P(), P(None, TGT, None, None, "src", None))
    out_specs = (P(None, AXES, None), P(None, TGT, "src"))
    return jax.shard_map(per_device, mesh=torus, in_specs=in_specs, out_specs=out_specs, check_vma=False)
```

```python
import functools
import math

import jax
import jax.numpy as jnp
from jax import lax
from jax.experimental import pallas as pl
from jax.experimental.pallas import tpu as pltpu
from jax.sharding import Mesh
from jax.sharding import PartitionSpec as P

AXES = ("tgt_0", "tgt_1", "tgt_2", "tgt_3", "src")
TGT = AXES[:4]
LINE = ("tgt_2", "tgt_3", "src")
PLANE = ("tgt_0", "tgt_1")
N_LINE = 16
N_PLANE = 32
SOURCES = N_PLANE * 128
LINE_SOURCES = N_LINE * 128
CHUNKS = ((0, 1), (4, 5), (24, 2))
WIDE = 4
BROAD = 16
ROW_SOURCES = 256
ROWS = (((0,), (0,)), ((), ()))

F32 = jnp.float32
BF16 = jnp.bfloat16
scale = 20.0
mobility = scale / (8.0 * math.pi)


def three_parts(x):
    high = x.astype(BF16).astype(F32)
    rest = x - high
    middle = rest.astype(BF16).astype(F32)
    low = (rest - middle).astype(BF16).astype(F32)
    return high, middle, low


def rows_of(x):
    return lax.broadcasted_iota(jnp.int32, x.shape, 0)


def left_rows(x, level):
    row = rows_of(x)
    a, b, c = three_parts(x)
    p, q, r = three_parts(level)
    first = jnp.where(row < 3, a, jnp.where(row == 3, p, jnp.where(row == 4, q, jnp.where(row == 5, r, 1.0))))
    second = jnp.where(row < 3, a, jnp.where(row == 3, 1.0, pltpu.roll(b, 4, 0)))
    return jnp.concatenate([first, second, b + pltpu.roll(a, 4, 0), c], axis=0).astype(BF16)


def right_rows(x, ones, level):
    row = rows_of(x)
    a, b, c = three_parts(x)
    p, q, r = three_parts(level)
    first = jnp.where(row < 3, a, jnp.where(row < 6, ones, jnp.where(row == 6, p, q)))
    second = jnp.where(row < 3, b, jnp.where(row == 3, r, pltpu.roll(a, 4, 0)))
    return jnp.concatenate([first, second, b + pltpu.roll(c, 4, 0), a], axis=0).astype(BF16)


def source_features(places, pushes):
    row = rows_of(places)
    center = jnp.mean(places, axis=1, keepdims=True)
    places = jnp.where(row < 3, (places - center) * scale, 0.0)
    pushes = jnp.where(row < 3, pushes, 0.0)
    square = jnp.sum(places * places, axis=0, keepdims=True)
    along = jnp.sum(places * pushes, axis=0, keepdims=True)
    a, b, _ = three_parts(pushes)
    push_rows = jnp.concatenate([a, b], axis=0).astype(BF16)
    y, g = places[0:3], pushes[0:3]
    form = jnp.concatenate(
        [g, along, along * y, g[2:3] * y[2:3], g[0:1] * y, g[1:2] * y, g[2:3] * y[0:2]], axis=0
    )
    form_rows = jnp.concatenate(three_parts(form), axis=0).astype(BF16)
    center = jnp.broadcast_to(center, (8, 128))
    return right_rows(-2.0 * places, 1.0, square), push_rows, form_rows, center


def pair_sums(targets, count, dist_ref, push_ref, form_ref, center_ref, step, unroll, fine):
    row = rows_of(targets)
    x = jnp.where(row < 3, (targets - center_ref[:, 0:1]) * scale, 0.0)
    square = jnp.sum(x * x, axis=0, keepdims=True) + 1.0
    features = left_rows(x, square)
    width = features.shape[1]

    def add_block(k, sums):
        root_sum, cube_sum = sums
        part = pl.ds(pl.multiple_of(k * step, step), step)
        dist_sq = lax.dot_general(dist_ref[:, part], features, ROWS, preferred_element_type=F32)
        root = lax.rsqrt(dist_sq)
        high = root.astype(BF16)
        root_sum += jnp.dot(push_ref[:, part], high, preferred_element_type=F32)
        if fine:
            low = (root - high.astype(F32)).astype(BF16)
            root_sum += jnp.dot(push_ref[:, part], low, preferred_element_type=F32)
        cube = root * root * root
        high = cube.astype(BF16)
        cube_sum += jnp.dot(form_ref[:, part], high, preferred_element_type=F32)
        if fine:
            low = (cube - high.astype(F32)).astype(BF16)
            cube_sum += jnp.dot(form_ref[:, part], low, preferred_element_type=F32)
        return root_sum, cube_sum

    start = (jnp.zeros((16, width), F32), jnp.zeros((48, width), F32))
    root_sum, cube_sum = lax.fori_loop(0, count // step, add_block, start, unroll=unroll)
    form = cube_sum[0:16] + cube_sum[16:32] + cube_sum[32:48]
    x0, x1, x2 = x[0:1], x[1:2], x[2:3]
    pull = x0 * form[0:1] + x1 * form[1:2] + x2 * form[2:3] - form[3:4]
    last = jnp.concatenate([form[14:16], form[7:8]], axis=0)
    moved = x0 * form[8:11] + x1 * form[11:14] + x2 * last - form[4:7]
    flow = root_sum[0:3] + root_sum[8:11] + form[0:3] + (x[0:3] * pull - moved)
    return jnp.concatenate([flow * mobility, jnp.zeros((5, width), F32)], axis=0)


def side_by_side(ref, first, count):
    return jnp.concatenate([ref[first + i] for i in range(count)], axis=1)


def packed(tiles, first_row):
    row = rows_of(tiles[0])
    lane = lax.broadcasted_iota(jnp.int32, tiles[0].shape, 1)
    keep = (row >= first_row) & (row < first_row + 3) & (lane < 16)
    blocks = []
    for start in range(0, len(tiles), 8):
        block = jnp.zeros_like(tiles[0])
        for i, tile in enumerate(tiles[start : start + 8]):
            piece = jnp.where(keep, tile, 0.0)
            block += pltpu.roll(piece, 16 * i, 1) if i else piece
        blocks.append(pltpu.roll(block, 8 - first_row, 0) if first_row else block)
    return jnp.concatenate(blocks, axis=1)


def own_kernel(fibre_ref, shell_ref, line_ref, plane_ref):
    fibre = jnp.concatenate([fibre_ref[:, 0, :], fibre_ref[:, 1, :]], axis=1)
    shell = jnp.concatenate([shell_ref[:, 0, :], jnp.zeros((3, 112), F32)], axis=1)
    tile = jnp.concatenate([fibre, shell, jnp.zeros((2, 128), F32)], axis=0)
    line_ref[...] = jnp.broadcast_to(tile[None], line_ref.shape)
    plane_ref[...] = jnp.broadcast_to(tile[None], plane_ref.shape)


def source_kernel(tiles_ref, bending_ref, dist_ref, push_ref, form_ref, center_ref):
    count = tiles_ref.shape[0]
    square = bending_ref[...]
    zero = jnp.zeros_like(square)
    both = jnp.concatenate(
        [jnp.concatenate([square, zero], axis=1), jnp.concatenate([zero, square], axis=1)], axis=0
    )
    pushes = -lax.dot_general(
        tiles_ref[...].reshape(count * 8, 128),
        both,
        (((1,), (1,)), ((), ())),
        precision=lax.Precision.HIGHEST,
        preferred_element_type=F32,
    )
    pushes = jnp.concatenate([pushes[8 * i : 8 * i + 8] for i in range(count)], axis=1)
    places = side_by_side(tiles_ref, 0, count)
    dist_ref[...], push_ref[...], form_ref[...], center_ref[...] = source_features(places, pushes)


def shell_kernel(line_ref, dist_ref, push_ref, form_ref, center_ref, part_ref, shell_ref):
    shell_ref[...] = packed([line_ref[i] for i in range(N_LINE)], 3)
    order = [pair * 4 + src for src in range(4) for pair in range(4)]
    targets = packed([line_ref[i] for i in order], 3)
    flow = pair_sums(targets, SOURCES, dist_ref, push_ref, form_ref, center_ref, 1024, 4, True)
    for src in range(4):
        half = flow[:, 128 * (src // 2) : 128 * (src // 2) + 128]
        piece = pltpu.roll(half, 64, 1) if src % 2 else half
        for pair in range(4):
            part_ref[pair * 4 + src] = piece


def fibre_kernel(first, parts, plane_ref, dist_ref, push_ref, form_ref, center_ref, flow_ref):
    for part in range(parts):
        flow = pair_sums(
            side_by_side(plane_ref, first + part * WIDE, WIDE),
            LINE_SOURCES,
            dist_ref,
            push_ref,
            form_ref,
            center_ref,
            1024,
            2,
            False,
        )
        for i in range(WIDE):
            flow_ref[part * WIDE + i] = flow[:, 128 * i : 128 * i + 128]


def total_of(parts_ref):
    total = parts_ref[0]
    for i in range(1, parts_ref.shape[0]):
        total += parts_ref[i]
    return total


def columns_kernel(parts_ref, out_ref):
    total = total_of(parts_ref)
    total = total.astype(BF16).astype(F32)
    out_ref[...] = jnp.broadcast_to(total[None], out_ref.shape)


def density_kernel(pair_ref, columns_ref, inverse_ref, out_ref):
    columns = jnp.concatenate([columns_ref[:, c, :] for c in range(3)], axis=1).astype(BF16)
    here = lax.broadcasted_iota(jnp.int32, (N_PLANE, 512), 0)
    there = lax.broadcasted_iota(jnp.int32, (N_PLANE, 512), 1)
    pick = (there % 128 == 4 * here + there // 128).astype(F32).astype(BF16)
    spread = lax.dot_general(columns, pick, ROWS, preferred_element_type=F32)
    parts = []
    for c in range(3):
        part = jnp.zeros((16, 128), F32)
        for pair in range(4):
            first = 128 * c + 16 * pair
            part += spread[first : first + 16, 128 * pair : 128 * pair + 128]
        parts.append(part)
    ones = jnp.ones((8, 128), F32)
    row = lax.broadcasted_iota(jnp.int32, (8, 64), 0)
    density = jnp.zeros((8, 64), F32)
    for x in range(3):
        total = jnp.zeros((64, 8, 128), F32)
        for c in range(3):
            block = inverse_ref[x, 0, :, c].astype(F32) * parts[c][None]
            total += block[:, 0:8] + block[:, 8:16]
        sums = jnp.sum(total, axis=1)
        line = lax.dot_general(
            ones, sums, (((1,), (1,)), ((), ())), precision=lax.Precision.HIGHEST, preferred_element_type=F32
        )
        density -= jnp.where(row == x, line, 0.0)
    density = jnp.concatenate([density, jnp.zeros((8, 64), F32)], axis=1)
    row = rows_of(density)
    lane = lax.broadcasted_iota(jnp.int32, density.shape, 1)
    lower = pltpu.roll(density, 3, 0)
    for src in range(4):
        piece = pltpu.roll(lower, 128 - 16 * src, 1) if src else lower
        piece = jnp.where((row >= 3) & (lane < 16), piece, 0.0)
        for pair in range(4):
            mine = (pair_ref[0] == pair).astype(F32)
            out_ref[pair * 4 + src] = density + mine * piece


def back_kernel(parts_ref, shell_ref, plane_ref, *refs):
    flows, refs = refs[: len(CHUNKS)], refs[len(CHUNKS) :]
    part_ref, density_ref, dist_ref, push_ref, form_ref, center_ref = refs
    lane = lax.broadcasted_iota(jnp.int32, (8, 128), 1)
    pairs = []
    for pair in range(4):
        total = parts_ref[pair * 4]
        for src in range(1, 4):
            total += parts_ref[pair * 4 + src]
        pairs.append(total)
    whole = (pairs[0] + pairs[1]) + (pairs[2] + pairs[3])
    density_ref[:, 0, :] = whole[3:6, 0:16]
    halves = [
        jnp.where(lane < 64, pairs[i], pltpu.roll(pairs[i + 1], 64, 1)) for i in (0, 2)
    ]
    dist_ref[...], push_ref[...], form_ref[...], center_ref[...] = source_features(
        shell_ref[...], jnp.concatenate(halves, axis=1)
    )
    fibre = [flow_ref[i] for flow_ref in flows for i in range(flow_ref.shape[0])]
    for index in range(0, N_PLANE, BROAD):
        flow = pair_sums(
            side_by_side(plane_ref, index, BROAD),
            ROW_SOURCES,
            dist_ref,
            push_ref,
            form_ref,
            center_ref,
            ROW_SOURCES,
            1,
            False,
        )
        for i in range(BROAD):
            part_ref[index + i] = flow[:, 128 * i : 128 * i + 128] + fibre[index + i]


def velocity_kernel(parts_ref, out_ref):
    total = total_of(parts_ref)
    out_ref[:, 0, :] = total[0:3, 0:64]
    out_ref[:, 1, :] = total[0:3, 64:128]


def tiles(count):
    return jax.ShapeDtypeStruct((count, 8, 128), F32)


def cost(pairs):
    return pl.CostEstimate(flops=pairs * 400, bytes_accessed=1 << 20, transcendentals=pairs)


def params(mib):
    return pltpu.CompilerParams(vmem_limit_bytes=mib << 20)


def feature_shapes(count):
    return [((32, count), BF16), ((16, count), BF16), ((48, count), BF16), ((8, 128), F32)]


def exchange(x, axes):
    return lax.all_to_all(x, axes, 0, 0, tiled=True)


def per_device(fibre_points, shell_points, bending, shell_inverse):
    own_line, own_plane = pl.pallas_call(
        own_kernel, out_shape=[tiles(N_LINE), tiles(N_PLANE)], compiler_params=params(62)
    )(fibre_points, shell_points)
    plane = exchange(own_plane, PLANE)
    own_line, _ = lax.optimization_barrier((own_line, plane))

    def features_of(x):
        count = x.shape[0] * 128
        return pl.pallas_call(
            source_kernel,
            out_shape=[jax.ShapeDtypeStruct(s, t) for s, t in feature_shapes(count)],
            compiler_params=params(24),
            cost_estimate=cost(64 * count),
        )(x, bending)

    features = features_of(plane)
    line, features = lax.optimization_barrier((exchange(own_line, LINE), features))
    shell_part, shell_places = pl.pallas_call(
        shell_kernel,
        out_shape=[tiles(N_LINE), jax.ShapeDtypeStruct((8, 256), F32)],
        compiler_params=params(24),
        cost_estimate=cost(256 * SOURCES),
    )(line, *features)
    held, _ = lax.optimization_barrier((line, shell_part))
    features = features_of(held)
    flows = []

    def exchange_beside(x, axes):
        first, parts = CHUNKS[len(flows)]
        held, _ = lax.optimization_barrier((plane, x))
        flow = pl.pallas_call(
            functools.partial(fibre_kernel, first, parts),
            out_shape=tiles(parts * WIDE),
            compiler_params=params(24),
            cost_estimate=cost(parts * WIDE * 128 * LINE_SOURCES),
        )(held, *features)
        x, flow = lax.optimization_barrier((exchange(x, axes), flow))
        flows.append(flow)
        return x

    shell_own = pl.pallas_call(
        columns_kernel, out_shape=tiles(N_PLANE), compiler_params=params(2)
    )(exchange_beside(shell_part, LINE))
    shell_all = exchange_beside(shell_own, PLANE)
    pair = lax.axis_index("tgt_2") * 2 + lax.axis_index("tgt_3")
    message = pl.pallas_call(
        density_kernel,
        out_shape=tiles(N_LINE),
        in_specs=[pl.BlockSpec(memory_space=pltpu.SMEM)] + [pl.BlockSpec(memory_space=pltpu.VMEM)] * 2,
        compiler_params=params(12),
    )(pair.astype(jnp.int32).reshape(1), shell_all, shell_inverse)
    density_parts = exchange_beside(message, LINE)
    part, density = pl.pallas_call(
        back_kernel,
        out_shape=[tiles(N_PLANE), jax.ShapeDtypeStruct((3, 1, 16), F32)],
        scratch_shapes=[pltpu.VMEM(s, t) for s, t in feature_shapes(ROW_SOURCES)],
        compiler_params=params(24),
        cost_estimate=cost(ROW_SOURCES * SOURCES),
    )(density_parts, shell_places, plane, *flows)
    velocity = pl.pallas_call(
        velocity_kernel, out_shape=jax.ShapeDtypeStruct((3, 2, 64), F32), compiler_params=params(2)
    )(exchange(part, PLANE))
    return velocity, density


def solution(mesh):
    torus = Mesh(mesh.devices.reshape(4, 8, 2, 2, mesh.shape["src"]), AXES)
    in_specs = (P(None, AXES, None), P(None, TGT, "src"), P(), P(None, TGT, None, None, "src", None))
    out_specs = (P(None, AXES, None), P(None, TGT, "src"))
    return jax.shard_map(per_device, mesh=torus, in_specs=in_specs, out_specs=out_specs, check_vma=False)
```

```python
import functools
import math

import jax
import jax.numpy as jnp
from jax import lax
from jax.experimental import pallas as pl
from jax.experimental.pallas import tpu as pltpu
from jax.sharding import Mesh
from jax.sharding import PartitionSpec as P

AXES = ("tgt_0", "tgt_1", "tgt_2", "tgt_3", "src")
TGT = AXES[:4]
LINE = ("tgt_2", "tgt_3", "src")
PLANE = ("tgt_0", "tgt_1")
N_LINE = 16
N_PLANE = 32
SOURCES = N_PLANE * 128
LINE_SOURCES = N_LINE * 128
CHUNKS = ((0, 1, 4, 1024), (4, 2, 10, 512), (24, 1, 8, 512))
BROAD = 16
ROW_SOURCES = 256
ROWS = (((0,), (0,)), ((), ()))

F32 = jnp.float32
BF16 = jnp.bfloat16
scale = 20.0
mobility = scale / (8.0 * math.pi)


def three_parts(x):
    high = x.astype(BF16).astype(F32)
    rest = x - high
    middle = rest.astype(BF16).astype(F32)
    low = (rest - middle).astype(BF16).astype(F32)
    return high, middle, low


def rows_of(x):
    return lax.broadcasted_iota(jnp.int32, x.shape, 0)


def left_rows(x, level):
    row = rows_of(x)
    a, b, c = three_parts(x)
    p, q, r = three_parts(level)
    first = jnp.where(row < 3, a, jnp.where(row == 3, p, jnp.where(row == 4, q, jnp.where(row == 5, r, 1.0))))
    second = jnp.where(row < 3, a, jnp.where(row == 3, 1.0, pltpu.roll(b, 4, 0)))
    return jnp.concatenate([first, second, b + pltpu.roll(a, 4, 0), c], axis=0).astype(BF16)


def right_rows(x, ones, level):
    row = rows_of(x)
    a, b, c = three_parts(x)
    p, q, r = three_parts(level)
    first = jnp.where(row < 3, a, jnp.where(row < 6, ones, jnp.where(row == 6, p, q)))
    second = jnp.where(row < 3, b, jnp.where(row == 3, r, pltpu.roll(a, 4, 0)))
    return jnp.concatenate([first, second, b + pltpu.roll(c, 4, 0), a], axis=0).astype(BF16)


def source_features(places, pushes):
    row = rows_of(places)
    center = jnp.mean(places, axis=1, keepdims=True)
    places = jnp.where(row < 3, (places - center) * scale, 0.0)
    pushes = jnp.where(row < 3, pushes, 0.0)
    square = jnp.sum(places * places, axis=0, keepdims=True)
    along = jnp.sum(places * pushes, axis=0, keepdims=True)
    a, b, _ = three_parts(pushes)
    push_rows = jnp.concatenate([a, b], axis=0).astype(BF16)
    y, g = places[0:3], pushes[0:3]
    form = jnp.concatenate(
        [g, along, along * y, g[2:3] * y[2:3], g[0:1] * y, g[1:2] * y, g[2:3] * y[0:2]], axis=0
    )
    form_rows = jnp.concatenate(three_parts(form), axis=0).astype(BF16)
    center = jnp.broadcast_to(center, (8, 128))
    return right_rows(-2.0 * places, 1.0, square), push_rows, form_rows, center


def pair_sums(targets, count, dist_ref, push_ref, form_ref, center_ref, step, unroll, fine):
    row = rows_of(targets)
    x = jnp.where(row < 3, (targets - center_ref[:, 0:1]) * scale, 0.0)
    square = jnp.sum(x * x, axis=0, keepdims=True) + 1.0
    features = left_rows(x, square)
    width = features.shape[1]

    def add_block(k, sums):
        root_sum, cube_sum = sums
        part = pl.ds(pl.multiple_of(k * step, step), step)
        dist_sq = lax.dot_general(dist_ref[:, part], features, ROWS, preferred_element_type=F32)
        root = lax.rsqrt(dist_sq)
        high = root.astype(BF16)
        root_sum += jnp.dot(push_ref[:, part], high, preferred_element_type=F32)
        if fine:
            low = (root - high.astype(F32)).astype(BF16)
            root_sum += jnp.dot(push_ref[:, part], low, preferred_element_type=F32)
        cube = root * root * root
        high = cube.astype(BF16)
        cube_sum += jnp.dot(form_ref[:, part], high, preferred_element_type=F32)
        if fine:
            low = (cube - high.astype(F32)).astype(BF16)
            cube_sum += jnp.dot(form_ref[:, part], low, preferred_element_type=F32)
        return root_sum, cube_sum

    start = (jnp.zeros((16, width), F32), jnp.zeros((48, width), F32))
    root_sum, cube_sum = lax.fori_loop(0, count // step, add_block, start, unroll=unroll)
    form = cube_sum[0:16] + cube_sum[16:32] + cube_sum[32:48]
    x0, x1, x2 = x[0:1], x[1:2], x[2:3]
    pull = x0 * form[0:1] + x1 * form[1:2] + x2 * form[2:3] - form[3:4]
    last = jnp.concatenate([form[14:16], form[7:8]], axis=0)
    moved = x0 * form[8:11] + x1 * form[11:14] + x2 * last - form[4:7]
    flow = root_sum[0:3] + root_sum[8:11] + form[0:3] + (x[0:3] * pull - moved)
    return jnp.concatenate([flow * mobility, jnp.zeros((5, width), F32)], axis=0)


def side_by_side(ref, first, count):
    return jnp.concatenate([ref[first + i] for i in range(count)], axis=1)


def packed(tiles, first_row):
    row = rows_of(tiles[0])
    lane = lax.broadcasted_iota(jnp.int32, tiles[0].shape, 1)
    keep = (row >= first_row) & (row < first_row + 3) & (lane < 16)
    blocks = []
    for start in range(0, len(tiles), 8):
        block = jnp.zeros_like(tiles[0])
        for i, tile in enumerate(tiles[start : start + 8]):
            piece = jnp.where(keep, tile, 0.0)
            block += pltpu.roll(piece, 16 * i, 1) if i else piece
        blocks.append(pltpu.roll(block, 8 - first_row, 0) if first_row else block)
    return jnp.concatenate(blocks, axis=1)


def own_kernel(fibre_ref, shell_ref, line_ref, plane_ref):
    fibre = jnp.concatenate([fibre_ref[:, 0, :], fibre_ref[:, 1, :]], axis=1)
    shell = jnp.concatenate([shell_ref[:, 0, :], jnp.zeros((3, 112), F32)], axis=1)
    tile = jnp.concatenate([fibre, shell, jnp.zeros((2, 128), F32)], axis=0)
    line_ref[...] = jnp.broadcast_to(tile[None], line_ref.shape)
    plane_ref[...] = jnp.broadcast_to(tile[None], plane_ref.shape)


def source_kernel(tiles_ref, bending_ref, dist_ref, push_ref, form_ref, center_ref):
    count = tiles_ref.shape[0]
    square = bending_ref[...]
    zero = jnp.zeros_like(square)
    both = jnp.concatenate(
        [jnp.concatenate([square, zero], axis=1), jnp.concatenate([zero, square], axis=1)], axis=0
    )
    pushes = -lax.dot_general(
        tiles_ref[...].reshape(count * 8, 128),
        both,
        (((1,), (1,)), ((), ())),
        precision=lax.Precision.HIGHEST,
        preferred_element_type=F32,
    )
    pushes = jnp.concatenate([pushes[8 * i : 8 * i + 8] for i in range(count)], axis=1)
    places = side_by_side(tiles_ref, 0, count)
    dist_ref[...], push_ref[...], form_ref[...], center_ref[...] = source_features(places, pushes)


def shell_kernel(line_ref, dist_ref, push_ref, form_ref, center_ref, part_ref, shell_ref):
    shell_ref[...] = packed([line_ref[i] for i in range(N_LINE)], 3)
    order = [pair * 4 + src for src in range(4) for pair in range(4)]
    targets = packed([line_ref[i] for i in order], 3)
    flow = pair_sums(targets, SOURCES, dist_ref, push_ref, form_ref, center_ref, 1024, 4, True)
    for src in range(4):
        half = flow[:, 128 * (src // 2) : 128 * (src // 2) + 128]
        piece = pltpu.roll(half, 64, 1) if src % 2 else half
        for pair in range(4):
            part_ref[pair * 4 + src] = piece


def fibre_kernel(chunk, plane_ref, dist_ref, push_ref, form_ref, center_ref, flow_ref):
    first, parts, wide, step = chunk
    for part in range(parts):
        flow = pair_sums(
            side_by_side(plane_ref, first + part * wide, wide),
            LINE_SOURCES,
            dist_ref,
            push_ref,
            form_ref,
            center_ref,
            step,
            2048 // step,
            False,
        )
        for i in range(wide):
            flow_ref[part * wide + i] = flow[:, 128 * i : 128 * i + 128]


def total_of(parts_ref):
    total = parts_ref[0]
    for i in range(1, parts_ref.shape[0]):
        total += parts_ref[i]
    return total


def columns_kernel(parts_ref, out_ref):
    total = total_of(parts_ref)
    total = total.astype(BF16).astype(F32)
    out_ref[...] = jnp.broadcast_to(total[None], out_ref.shape)


def density_kernel(pair_ref, columns_ref, inverse_ref, out_ref):
    columns = jnp.concatenate([columns_ref[:, c, :] for c in range(3)], axis=1).astype(BF16)
    here = lax.broadcasted_iota(jnp.int32, (N_PLANE, 512), 0)
    there = lax.broadcasted_iota(jnp.int32, (N_PLANE, 512), 1)
    pick = (there % 128 == 4 * here + there // 128).astype(F32).astype(BF16)
    spread = lax.dot_general(columns, pick, ROWS, preferred_element_type=F32)
    parts = []
    for c in range(3):
        part = jnp.zeros((16, 128), F32)
        for pair in range(4):
            first = 128 * c + 16 * pair
            part += spread[first : first + 16, 128 * pair : 128 * pair + 128]
        parts.append(part)
    ones = jnp.ones((8, 128), F32)
    row = lax.broadcasted_iota(jnp.int32, (8, 64), 0)
    density = jnp.zeros((8, 64), F32)
    for x in range(3):
        total = jnp.zeros((64, 8, 128), F32)
        for c in range(3):
            block = inverse_ref[x, 0, :, c].astype(F32) * parts[c][None]
            total += block[:, 0:8] + block[:, 8:16]
        sums = jnp.sum(total, axis=1)
        line = lax.dot_general(
            ones, sums, (((1,), (1,)), ((), ())), precision=lax.Precision.HIGHEST, preferred_element_type=F32
        )
        density -= jnp.where(row == x, line, 0.0)
    density = jnp.concatenate([density, jnp.zeros((8, 64), F32)], axis=1)
    row = rows_of(density)
    lane = lax.broadcasted_iota(jnp.int32, density.shape, 1)
    lower = pltpu.roll(density, 3, 0)
    for src in range(4):
        piece = pltpu.roll(lower, 128 - 16 * src, 1) if src else lower
        piece = jnp.where((row >= 3) & (lane < 16), piece, 0.0)
        for pair in range(4):
            mine = (pair_ref[0] == pair).astype(F32)
            out_ref[pair * 4 + src] = density + mine * piece


def back_kernel(parts_ref, shell_ref, plane_ref, *refs):
    flows, refs = refs[: len(CHUNKS)], refs[len(CHUNKS) :]
    part_ref, density_ref, dist_ref, push_ref, form_ref, center_ref = refs
    lane = lax.broadcasted_iota(jnp.int32, (8, 128), 1)
    pairs = []
    for pair in range(4):
        total = parts_ref[pair * 4]
        for src in range(1, 4):
            total += parts_ref[pair * 4 + src]
        pairs.append(total)
    whole = (pairs[0] + pairs[1]) + (pairs[2] + pairs[3])
    density_ref[:, 0, :] = whole[3:6, 0:16]
    halves = [
        jnp.where(lane < 64, pairs[i], pltpu.roll(pairs[i + 1], 64, 1)) for i in (0, 2)
    ]
    dist_ref[...], push_ref[...], form_ref[...], center_ref[...] = source_features(
        shell_ref[...], jnp.concatenate(halves, axis=1)
    )
    fibre = [flow_ref[i] for flow_ref in flows for i in range(flow_ref.shape[0])]
    for index in range(0, N_PLANE, BROAD):
        flow = pair_sums(
            side_by_side(plane_ref, index, BROAD),
            ROW_SOURCES,
            dist_ref,
            push_ref,
            form_ref,
            center_ref,
            ROW_SOURCES,
            1,
            False,
        )
        for i in range(BROAD):
            part_ref[index + i] = flow[:, 128 * i : 128 * i + 128] + fibre[index + i]


def velocity_kernel(parts_ref, out_ref):
    total = total_of(parts_ref)
    out_ref[:, 0, :] = total[0:3, 0:64]
    out_ref[:, 1, :] = total[0:3, 64:128]


def tiles(count):
    return jax.ShapeDtypeStruct((count, 8, 128), F32)


def cost(pairs):
    return pl.CostEstimate(flops=pairs * 400, bytes_accessed=1 << 20, transcendentals=pairs)


def params(mib):
    return pltpu.CompilerParams(vmem_limit_bytes=mib << 20)


def feature_shapes(count):
    return [((32, count), BF16), ((16, count), BF16), ((48, count), BF16), ((8, 128), F32)]


def exchange(x, axes):
    return lax.all_to_all(x, axes, 0, 0, tiled=True)


def per_device(fibre_points, shell_points, bending, shell_inverse):
    own_line, own_plane = pl.pallas_call(
        own_kernel, out_shape=[tiles(N_LINE), tiles(N_PLANE)], compiler_params=params(62)
    )(fibre_points, shell_points)
    plane = exchange(own_plane, PLANE)
    own_line, _ = lax.optimization_barrier((own_line, plane))

    def features_of(x):
        count = x.shape[0] * 128
        return pl.pallas_call(
            source_kernel,
            out_shape=[jax.ShapeDtypeStruct(s, t) for s, t in feature_shapes(count)],
            compiler_params=params(24),
            cost_estimate=cost(64 * count),
        )(x, bending)

    features = features_of(plane)
    line, features = lax.optimization_barrier((exchange(own_line, LINE), features))
    shell_part, shell_places = pl.pallas_call(
        shell_kernel,
        out_shape=[tiles(N_LINE), jax.ShapeDtypeStruct((8, 256), F32)],
        compiler_params=params(24),
        cost_estimate=cost(256 * SOURCES),
    )(line, *features)
    held, _ = lax.optimization_barrier((line, shell_part))
    features = features_of(held)
    flows = []

    def exchange_beside(x, axes):
        chunk = CHUNKS[len(flows)]
        count = chunk[1] * chunk[2]
        held, _ = lax.optimization_barrier((plane, x))
        flow = pl.pallas_call(
            functools.partial(fibre_kernel, chunk),
            out_shape=tiles(count),
            compiler_params=params(24),
            cost_estimate=cost(count * 128 * LINE_SOURCES),
        )(held, *features)
        x, flow = lax.optimization_barrier((exchange(x, axes), flow))
        flows.append(flow)
        return x

    shell_own = pl.pallas_call(
        columns_kernel, out_shape=tiles(N_PLANE), compiler_params=params(2)
    )(exchange_beside(shell_part, LINE))
    shell_all = exchange_beside(shell_own, PLANE)
    pair = lax.axis_index("tgt_2") * 2 + lax.axis_index("tgt_3")
    message = pl.pallas_call(
        density_kernel,
        out_shape=tiles(N_LINE),
        in_specs=[pl.BlockSpec(memory_space=pltpu.SMEM)] + [pl.BlockSpec(memory_space=pltpu.VMEM)] * 2,
        compiler_params=params(12),
    )(pair.astype(jnp.int32).reshape(1), shell_all, shell_inverse)
    density_parts = exchange_beside(message, LINE)
    part, density = pl.pallas_call(
        back_kernel,
        out_shape=[tiles(N_PLANE), jax.ShapeDtypeStruct((3, 1, 16), F32)],
        scratch_shapes=[pltpu.VMEM(s, t) for s, t in feature_shapes(ROW_SOURCES)],
        compiler_params=params(24),
        cost_estimate=cost(ROW_SOURCES * SOURCES),
    )(density_parts, shell_places, plane, *flows)
    velocity = pl.pallas_call(
        velocity_kernel, out_shape=jax.ShapeDtypeStruct((3, 2, 64), F32), compiler_params=params(2)
    )(exchange(part, PLANE))
    return velocity, density


def solution(mesh):
    torus = Mesh(mesh.devices.reshape(4, 8, 2, 2, mesh.shape["src"]), AXES)
    in_specs = (P(None, AXES, None), P(None, TGT, "src"), P(), P(None, TGT, None, None, "src", None))
    out_specs = (P(None, AXES, None), P(None, TGT, "src"))
    return jax.shard_map(per_device, mesh=torus, in_specs=in_specs, out_specs=out_specs, check_vma=False)
```

```python
import functools
import math

import jax
import jax.numpy as jnp
from jax import lax
from jax.experimental import pallas as pl
from jax.experimental.pallas import tpu as pltpu
from jax.sharding import Mesh
from jax.sharding import PartitionSpec as P

AXES = ("tgt_0", "tgt_1", "tgt_2", "tgt_3", "src")
TGT = AXES[:4]
LINE = ("tgt_2", "tgt_3", "src")
PLANE = ("tgt_0", "tgt_1")
N_LINE = 16
N_PLANE = 32
SOURCES = N_PLANE * 128
LINE_SOURCES = N_LINE * 128
CHUNKS = ((0, 2, 11, 512), (22, 1, 10, 512))
BROAD = 16
ROW_SOURCES = 256
ROWS = (((0,), (0,)), ((), ()))

F32 = jnp.float32
BF16 = jnp.bfloat16
scale = 20.0
mobility = scale / (8.0 * math.pi)


def three_parts(x):
    high = x.astype(BF16).astype(F32)
    rest = x - high
    middle = rest.astype(BF16).astype(F32)
    low = (rest - middle).astype(BF16).astype(F32)
    return high, middle, low


def rows_of(x):
    return lax.broadcasted_iota(jnp.int32, x.shape, 0)


def left_rows(x, level):
    row = rows_of(x)
    a, b, c = three_parts(x)
    p, q, r = three_parts(level)
    first = jnp.where(row < 3, a, jnp.where(row == 3, p, jnp.where(row == 4, q, jnp.where(row == 5, r, 1.0))))
    second = jnp.where(row < 3, a, jnp.where(row == 3, 1.0, pltpu.roll(b, 4, 0)))
    return jnp.concatenate([first, second, b + pltpu.roll(a, 4, 0), c], axis=0).astype(BF16)


def right_rows(x, ones, level):
    row = rows_of(x)
    a, b, c = three_parts(x)
    p, q, r = three_parts(level)
    first = jnp.where(row < 3, a, jnp.where(row < 6, ones, jnp.where(row == 6, p, q)))
    second = jnp.where(row < 3, b, jnp.where(row == 3, r, pltpu.roll(a, 4, 0)))
    return jnp.concatenate([first, second, b + pltpu.roll(c, 4, 0), a], axis=0).astype(BF16)


def source_features(places, pushes):
    row = rows_of(places)
    center = jnp.mean(places, axis=1, keepdims=True)
    places = jnp.where(row < 3, (places - center) * scale, 0.0)
    pushes = jnp.where(row < 3, pushes, 0.0)
    square = jnp.sum(places * places, axis=0, keepdims=True)
    along = jnp.sum(places * pushes, axis=0, keepdims=True)
    a, b, _ = three_parts(pushes)
    push_rows = jnp.concatenate([a, b], axis=0).astype(BF16)
    y, g = places[0:3], pushes[0:3]
    form = jnp.concatenate(
        [g, along, along * y, g[2:3] * y[2:3], g[0:1] * y, g[1:2] * y, g[2:3] * y[0:2]], axis=0
    )
    form_rows = jnp.concatenate(three_parts(form), axis=0).astype(BF16)
    center = jnp.broadcast_to(center, (8, 128))
    return right_rows(-2.0 * places, 1.0, square), push_rows, form_rows, center


def pair_sums(targets, count, dist_ref, push_ref, form_ref, center_ref, step, unroll, fine):
    row = rows_of(targets)
    x = jnp.where(row < 3, (targets - center_ref[:, 0:1]) * scale, 0.0)
    square = jnp.sum(x * x, axis=0, keepdims=True) + 1.0
    features = left_rows(x, square)
    width = features.shape[1]

    def add_block(k, sums):
        root_sum, cube_sum = sums
        part = pl.ds(pl.multiple_of(k * step, step), step)
        dist_sq = lax.dot_general(dist_ref[:, part], features, ROWS, preferred_element_type=F32)
        root = lax.rsqrt(dist_sq)
        high = root.astype(BF16)
        root_sum += jnp.dot(push_ref[:, part], high, preferred_element_type=F32)
        if fine:
            low = (root - high.astype(F32)).astype(BF16)
            root_sum += jnp.dot(push_ref[:, part], low, preferred_element_type=F32)
        cube = root * root * root
        high = cube.astype(BF16)
        cube_sum += jnp.dot(form_ref[:, part], high, preferred_element_type=F32)
        if fine:
            low = (cube - high.astype(F32)).astype(BF16)
            cube_sum += jnp.dot(form_ref[:, part], low, preferred_element_type=F32)
        return root_sum, cube_sum

    start = (jnp.zeros((16, width), F32), jnp.zeros((48, width), F32))
    root_sum, cube_sum = lax.fori_loop(0, count // step, add_block, start, unroll=unroll)
    form = cube_sum[0:16] + cube_sum[16:32] + cube_sum[32:48]
    x0, x1, x2 = x[0:1], x[1:2], x[2:3]
    pull = x0 * form[0:1] + x1 * form[1:2] + x2 * form[2:3] - form[3:4]
    last = jnp.concatenate([form[14:16], form[7:8]], axis=0)
    moved = x0 * form[8:11] + x1 * form[11:14] + x2 * last - form[4:7]
    flow = root_sum[0:3] + root_sum[8:11] + form[0:3] + (x[0:3] * pull - moved)
    return jnp.concatenate([flow * mobility, jnp.zeros((5, width), F32)], axis=0)


def side_by_side(ref, first, count):
    return jnp.concatenate([ref[first + i] for i in range(count)], axis=1)


def packed(tiles, first_row):
    row = rows_of(tiles[0])
    lane = lax.broadcasted_iota(jnp.int32, tiles[0].shape, 1)
    keep = (row >= first_row) & (row < first_row + 3) & (lane < 16)
    blocks = []
    for start in range(0, len(tiles), 8):
        block = jnp.zeros_like(tiles[0])
        for i, tile in enumerate(tiles[start : start + 8]):
            piece = jnp.where(keep, tile, 0.0)
            block += pltpu.roll(piece, 16 * i, 1) if i else piece
        blocks.append(pltpu.roll(block, 8 - first_row, 0) if first_row else block)
    return jnp.concatenate(blocks, axis=1)


def own_kernel(fibre_ref, shell_ref, line_ref, plane_ref):
    fibre = jnp.concatenate([fibre_ref[:, 0, :], fibre_ref[:, 1, :]], axis=1)
    shell = jnp.concatenate([shell_ref[:, 0, :], jnp.zeros((3, 112), F32)], axis=1)
    tile = jnp.concatenate([fibre, shell, jnp.zeros((2, 128), F32)], axis=0)
    line_ref[...] = jnp.broadcast_to(tile[None], line_ref.shape)
    plane_ref[...] = jnp.broadcast_to(tile[None], plane_ref.shape)


def source_kernel(tiles_ref, bending_ref, dist_ref, push_ref, form_ref, center_ref):
    count = tiles_ref.shape[0]
    square = bending_ref[...]
    zero = jnp.zeros_like(square)
    both = jnp.concatenate(
        [jnp.concatenate([square, zero], axis=1), jnp.concatenate([zero, square], axis=1)], axis=0
    )
    pushes = -lax.dot_general(
        tiles_ref[...].reshape(count * 8, 128),
        both,
        (((1,), (1,)), ((), ())),
        precision=lax.Precision.HIGHEST,
        preferred_element_type=F32,
    )
    pushes = jnp.concatenate([pushes[8 * i : 8 * i + 8] for i in range(count)], axis=1)
    places = side_by_side(tiles_ref, 0, count)
    dist_ref[...], push_ref[...], form_ref[...], center_ref[...] = source_features(places, pushes)


def shell_kernel(line_ref, dist_ref, push_ref, form_ref, center_ref, part_ref, shell_ref):
    shell_ref[...] = packed([line_ref[i] for i in range(N_LINE)], 3)
    order = [pair * 4 + src for src in range(4) for pair in range(4)]
    targets = packed([line_ref[i] for i in order], 3)
    flow = pair_sums(targets, SOURCES, dist_ref, push_ref, form_ref, center_ref, 1024, 4, True)
    for src in range(4):
        half = flow[:, 128 * (src // 2) : 128 * (src // 2) + 128]
        piece = pltpu.roll(half, 64, 1) if src % 2 else half
        for pair in range(4):
            part_ref[pair * 4 + src] = piece


def fibre_kernel(chunk, plane_ref, dist_ref, push_ref, form_ref, center_ref, flow_ref):
    first, parts, wide, step = chunk
    for part in range(parts):
        flow = pair_sums(
            side_by_side(plane_ref, first + part * wide, wide),
            LINE_SOURCES,
            dist_ref,
            push_ref,
            form_ref,
            center_ref,
            step,
            2048 // step,
            False,
        )
        for i in range(wide):
            flow_ref[part * wide + i] = flow[:, 128 * i : 128 * i + 128]


def total_of(parts_ref):
    total = parts_ref[0]
    for i in range(1, parts_ref.shape[0]):
        total += parts_ref[i]
    return total


def columns_kernel(parts_ref, out_ref):
    total = total_of(parts_ref)
    total = total.astype(BF16).astype(F32)
    out_ref[...] = jnp.broadcast_to(total[None], out_ref.shape)


def density_kernel(pair_ref, columns_ref, inverse_ref, out_ref):
    columns = jnp.concatenate([columns_ref[:, c, :] for c in range(3)], axis=1).astype(BF16)
    here = lax.broadcasted_iota(jnp.int32, (N_PLANE, 512), 0)
    there = lax.broadcasted_iota(jnp.int32, (N_PLANE, 512), 1)
    pick = (there % 128 == 4 * here + there // 128).astype(F32).astype(BF16)
    spread = lax.dot_general(columns, pick, ROWS, preferred_element_type=F32)
    parts = []
    for c in range(3):
        part = jnp.zeros((16, 128), F32)
        for pair in range(4):
            first = 128 * c + 16 * pair
            part += spread[first : first + 16, 128 * pair : 128 * pair + 128]
        parts.append(part)
    ones = jnp.ones((8, 128), F32)
    row = lax.broadcasted_iota(jnp.int32, (8, 64), 0)
    density = jnp.zeros((8, 64), F32)
    for x in range(3):
        total = jnp.zeros((64, 8, 128), F32)
        for c in range(3):
            block = inverse_ref[x, 0, :, c].astype(F32) * parts[c][None]
            total += block[:, 0:8] + block[:, 8:16]
        sums = jnp.sum(total, axis=1)
        line = lax.dot_general(
            ones, sums, (((1,), (1,)), ((), ())), precision=lax.Precision.HIGHEST, preferred_element_type=F32
        )
        density -= jnp.where(row == x, line, 0.0)
    density = jnp.concatenate([density, jnp.zeros((8, 64), F32)], axis=1)
    row = rows_of(density)
    lane = lax.broadcasted_iota(jnp.int32, density.shape, 1)
    lower = pltpu.roll(density, 3, 0)
    for src in range(4):
        piece = pltpu.roll(lower, 128 - 16 * src, 1) if src else lower
        piece = jnp.where((row >= 3) & (lane < 16), piece, 0.0)
        for pair in range(4):
            mine = (pair_ref[0] == pair).astype(F32)
            out_ref[pair * 4 + src] = density + mine * piece


def back_kernel(parts_ref, shell_ref, plane_ref, *refs):
    flows, refs = refs[: len(CHUNKS)], refs[len(CHUNKS) :]
    part_ref, density_ref, dist_ref, push_ref, form_ref, center_ref = refs
    lane = lax.broadcasted_iota(jnp.int32, (8, 128), 1)
    pairs = []
    for pair in range(4):
        total = parts_ref[pair * 4]
        for src in range(1, 4):
            total += parts_ref[pair * 4 + src]
        pairs.append(total)
    whole = (pairs[0] + pairs[1]) + (pairs[2] + pairs[3])
    density_ref[:, 0, :] = whole[3:6, 0:16]
    halves = [
        jnp.where(lane < 64, pairs[i], pltpu.roll(pairs[i + 1], 64, 1)) for i in (0, 2)
    ]
    dist_ref[...], push_ref[...], form_ref[...], center_ref[...] = source_features(
        shell_ref[...], jnp.concatenate(halves, axis=1)
    )
    fibre = [flow_ref[i] for flow_ref in flows for i in range(flow_ref.shape[0])]
    for index in range(0, N_PLANE, BROAD):
        flow = pair_sums(
            side_by_side(plane_ref, index, BROAD),
            ROW_SOURCES,
            dist_ref,
            push_ref,
            form_ref,
            center_ref,
            ROW_SOURCES,
            1,
            False,
        )
        for i in range(BROAD):
            part_ref[index + i] = flow[:, 128 * i : 128 * i + 128] + fibre[index + i]


def velocity_kernel(parts_ref, out_ref):
    total = total_of(parts_ref)
    out_ref[:, 0, :] = total[0:3, 0:64]
    out_ref[:, 1, :] = total[0:3, 64:128]


def tiles(count):
    return jax.ShapeDtypeStruct((count, 8, 128), F32)


def cost(pairs):
    return pl.CostEstimate(flops=pairs * 400, bytes_accessed=1 << 20, transcendentals=pairs)


def params(mib):
    return pltpu.CompilerParams(vmem_limit_bytes=mib << 20)


def feature_shapes(count):
    return [((32, count), BF16), ((16, count), BF16), ((48, count), BF16), ((8, 128), F32)]


def exchange(x, axes):
    return lax.all_to_all(x, axes, 0, 0, tiled=True)


def per_device(fibre_points, shell_points, bending, shell_inverse):
    own_line, own_plane = pl.pallas_call(
        own_kernel, out_shape=[tiles(N_LINE), tiles(N_PLANE)], compiler_params=params(62)
    )(fibre_points, shell_points)
    plane = exchange(own_plane, PLANE)
    own_line, _ = lax.optimization_barrier((own_line, plane))

    def features_of(x):
        count = x.shape[0] * 128
        return pl.pallas_call(
            source_kernel,
            out_shape=[jax.ShapeDtypeStruct(s, t) for s, t in feature_shapes(count)],
            compiler_params=params(24),
            cost_estimate=cost(64 * count),
        )(x, bending)

    features = features_of(plane)
    line, features = lax.optimization_barrier((exchange(own_line, LINE), features))
    shell_part, shell_places = pl.pallas_call(
        shell_kernel,
        out_shape=[tiles(N_LINE), jax.ShapeDtypeStruct((8, 256), F32)],
        compiler_params=params(24),
        cost_estimate=cost(256 * SOURCES),
    )(line, *features)
    shell_own = pl.pallas_call(
        columns_kernel, out_shape=tiles(N_PLANE), compiler_params=params(2)
    )(exchange(shell_part, LINE))
    held, _ = lax.optimization_barrier((line, shell_own))
    features = features_of(held)
    flows = []

    def exchange_beside(x, axes):
        chunk = CHUNKS[len(flows)]
        count = chunk[1] * chunk[2]
        held, _ = lax.optimization_barrier((plane, x))
        flow = pl.pallas_call(
            functools.partial(fibre_kernel, chunk),
            out_shape=tiles(count),
            compiler_params=params(24),
            cost_estimate=cost(count * 128 * LINE_SOURCES),
        )(held, *features)
        x, flow = lax.optimization_barrier((exchange(x, axes), flow))
        flows.append(flow)
        return x

    shell_all = exchange_beside(shell_own, PLANE)
    pair = lax.axis_index("tgt_2") * 2 + lax.axis_index("tgt_3")
    message = pl.pallas_call(
        density_kernel,
        out_shape=tiles(N_LINE),
        in_specs=[pl.BlockSpec(memory_space=pltpu.SMEM)] + [pl.BlockSpec(memory_space=pltpu.VMEM)] * 2,
        compiler_params=params(12),
    )(pair.astype(jnp.int32).reshape(1), shell_all, shell_inverse)
    density_parts = exchange_beside(message, LINE)
    part, density = pl.pallas_call(
        back_kernel,
        out_shape=[tiles(N_PLANE), jax.ShapeDtypeStruct((3, 1, 16), F32)],
        scratch_shapes=[pltpu.VMEM(s, t) for s, t in feature_shapes(ROW_SOURCES)],
        compiler_params=params(24),
        cost_estimate=cost(ROW_SOURCES * SOURCES),
    )(density_parts, shell_places, plane, *flows)
    velocity = pl.pallas_call(
        velocity_kernel, out_shape=jax.ShapeDtypeStruct((3, 2, 64), F32), compiler_params=params(2)
    )(exchange(part, PLANE))
    return velocity, density


def solution(mesh):
    torus = Mesh(mesh.devices.reshape(4, 8, 2, 2, mesh.shape["src"]), AXES)
    in_specs = (P(None, AXES, None), P(None, TGT, "src"), P(), P(None, TGT, None, None, "src", None))
    out_specs = (P(None, AXES, None), P(None, TGT, "src"))
    return jax.shard_map(per_device, mesh=torus, in_specs=in_specs, out_specs=out_specs, check_vma=False)
```
